32 devices in a mesh: space: 4 (over y, core), vel: 8 (over z, x).
Axes of the slice: x: 2, y: 2, z: 4, core: 2. Of those that a mesh axis runs over, the one named last changes fastest.
Arguments:
- distribution: float32 [32768, 16, 128], P('vel', 'space'), may hold values from -6 to 6
- velocity_order: int32 [32768], P('vel'), may hold values from 0 to 32767, as said below
- macro_state: float32 [13, 16, 128], P(None, 'space'), may hold values from -5 to 5
- rarefaction: float32 [16, 128], P('space'), may hold values from 0.1 to 3
- wall_mask: int32 [16, 128], P('space'), may hold values from 0 to 2, as said below
Outputs:
- dist_out: float32 [32768, 16, 128], P('vel', 'space')
- moments_out: float32 [13, 16, 128], P(None, 'space')
The draws below stay inside these ranges and needn't reach their ends.
Inputs may be any that keep to these rules, and one draw needn't show every extreme that they name: `velocity_order`: A permutation of the velocity indices. In each shard of 4096 consecutive slots along vel, the first 2048 slots hold indices of at least 16384 and the others indices below 16384. `wall_mask`: cells on the faces x = 0, x = 15, y = 0, z = 0 and z = 7 are 1; the other cells of the face y = 15 are 2; some interior cells are 1.
All inputs are finite; a program needn't handle non-finite values.
Results may differ from the reference program's by a relative error of at most 0.0003.
Values sent between devices are 32-bit elements; how exact they have to be, the bound alone decides.
A program may use at most 64 MiB of HBM per device.

```python
import math
import jax
import jax.numpy as jnp
from jax import lax

NQ = 32
NV = 32768
NY = 16
NZ = 8
SWEEPS = 4
NX = 16
N_VEL = 8


def draw_velocity_order(key, part):
    key = jax.random.fold_in(key, 11)
    upper_key, lower_key = jax.random.split(key)
    half_total = NQ * NQ * NQ // 2
    upper_half = jax.random.permutation(upper_key, half_total).astype(jnp.int32) + half_total
    lower_half = jax.random.permutation(lower_key, half_total).astype(jnp.int32)
    shard_rows = jnp.concatenate([upper_half.reshape(N_VEL, -1), lower_half.reshape(N_VEL, -1)], axis=1)
    return shard_rows.reshape(-1)


def draw_wall_mask(key, part):
    key = jax.random.fold_in(key, 23)
    x_index = jnp.arange(NX, dtype=jnp.int32)[:, None]
    flat_index = jnp.arange(NY * NZ, dtype=jnp.int32)[None, :]
    y_index = flat_index // NZ
    z_index = flat_index % NZ
    still_wall = (x_index == 0) | (x_index == NX - 1) | (y_index == 0) | (z_index == 0) | (z_index == NZ - 1)
    lid_cells = (y_index == NY - 1) & jnp.logical_not(still_wall)
    blocked = jax.random.randint(key, (NX, NY * NZ), 0, 16) == 0
    inner_mask = jnp.where(blocked, 1, 0)
    return jnp.where(still_wall, 1, jnp.where(lid_cells, 2, inner_mask)).astype(jnp.int32)


def shard_levels(own_key, extent, shards, smallest, high):
    factor_of, own = 1.0, jax.random.fold_in(own_key, 6)
    for dim, parts in shards:
        heights = jnp.exp(jax.random.uniform(jax.random.fold_in(own, dim), (parts,), jnp.float32, smallest / len(shards), high / len(shards)))
        factor_of = factor_of * jnp.repeat(heights, extent[dim] // parts).reshape([-1 if axis == dim else 1 for axis in range(len(extent))])
    return factor_of


def gaussian(key, extent, scale, reach, cuts=(), kind=jnp.bfloat16):
    factor_of = shard_levels(key, extent, cuts, -0.22, 0.18) if cuts else 1.0
    drawn = jax.random.normal(key, extent, jnp.float32) * scale * factor_of
    return jnp.minimum(jnp.maximum(drawn, -reach), reach).astype(kind)


def setup_inputs(seed: int = 0) -> dict:
    key_of = jax.random.split(jax.random.key(seed), 6)
    return {
        "distribution": gaussian(key_of[0], (NV, NX, NY * NZ), 1.0, 6.0, ((0, 8), (1, 4)), jnp.float32),
        "velocity_order": draw_velocity_order(jax.random.fold_in(key_of[5], 71), 0),
        "macro_state": gaussian(key_of[2], (13, NX, NY * NZ), 1.0, 5.0, ((1, 4),), jnp.float32),
        "rarefaction": jnp.clip(jnp.exp(math.log(3.0) - 3.4011974 * jax.random.uniform(key_of[3], (NX, NY * NZ), jnp.float32) ** shard_levels(key_of[3], (NX, NY * NZ), ((0, 4),), -0.2, 0.2)), 0.1, 3.0),
        "wall_mask": draw_wall_mask(jax.random.fold_in(key_of[5], 71), 0),
    }


VELOCITY_RANGE = 4.0
LID_SPEED = 1.0
DIFFUSION = 1.0
REACTION = 1.0
COUPLING = ((0, 1, 0, 0.24), (0, 2, 1, 0.24), (0, 3, 2, 0.24),
            (1, 0, 0, 0.2), (1, 4, 0, 0.2), (1, 5, 0, 0.2), (1, 7, 1, 0.1), (1, 8, 2, 0.1),
            (2, 0, 1, 0.2), (2, 4, 1, 0.2), (2, 6, 1, 0.2), (2, 7, 0, 0.1), (2, 9, 2, 0.1),
            (3, 0, 2, 0.2), (3, 4, 2, 0.2), (3, 8, 0, 0.1), (3, 9, 1, 0.1),
            (4, 10, 0, 0.2), (4, 11, 1, 0.2), (4, 12, 2, 0.2),
            (5, 1, 0, 0.4), (5, 10, 0, 0.2), (6, 2, 1, 0.4), (6, 11, 1, 0.2),
            (7, 1, 1, 0.2), (7, 2, 0, 0.2), (8, 1, 2, 0.2), (8, 3, 0, 0.2),
            (9, 2, 2, 0.2), (9, 3, 1, 0.2),
            (10, 4, 0, 0.5), (10, 5, 0, 0.2), (11, 4, 1, 0.5), (11, 6, 1, 0.2),
            (12, 4, 2, 0.5), (12, 8, 0, 0.1), (12, 9, 1, 0.1))


def coupling_tables(dtype):
    coupling_table = [[[0.0 for column_index in range(13)] for row_index in range(13)] for dim_index in range(3)]
    for row_index, column_index, dim_index, value in COUPLING:
        coupling_table[dim_index][row_index][column_index] = value
    return jnp.asarray(coupling_table, dtype=dtype)


def velocity_tables(velocity_order, points):
    order_int = velocity_order.astype(jnp.int32)
    first_index = order_int // (points * points)
    second_index = (order_int // points) % points
    third_index = order_int % points

    def velocity_axis(index_value):
        return VELOCITY_RANGE * (2.0 * index_value.astype(jnp.float32) + 1.0 - points) / points

    xi_x = velocity_axis(first_index)
    xi_y = velocity_axis(second_index)
    xi_z = velocity_axis(third_index)
    square = xi_x * xi_x + xi_y * xi_y + xi_z * xi_z
    quad_weight = (2.0 * VELOCITY_RANGE / points) ** 3 * jnp.exp(-square) / jnp.pi ** 1.5
    unit_row = jnp.ones_like(square)
    zero_row = jnp.zeros_like(square)
    energy = square - 1.5
    heat_factor = square - 2.5
    moment_rows = jnp.stack([unit_row, xi_x, xi_y, xi_z, (2.0 / 3.0) * energy,
                             2.0 * (xi_x * xi_x - square / 3.0), 2.0 * (xi_y * xi_y - square / 3.0),
                             2.0 * xi_x * xi_y, 2.0 * xi_x * xi_z, 2.0 * xi_y * xi_z,
                             xi_x * heat_factor, xi_y * heat_factor, xi_z * heat_factor]) * quad_weight[None]
    shakhov = 4.0 / 15.0
    equilibrium_rows = jnp.stack([unit_row, 2.0 * xi_x, 2.0 * xi_y, 2.0 * xi_z, energy,
                                  zero_row, zero_row, zero_row, zero_row, zero_row,
                                  shakhov * xi_x * heat_factor, shakhov * xi_y * heat_factor,
                                  shakhov * xi_z * heat_factor])
    grad_rows = jnp.stack([unit_row, 2.0 * xi_x, 2.0 * xi_y, 2.0 * xi_z, energy,
                           xi_x * xi_x - xi_z * xi_z, xi_y * xi_y - xi_z * xi_z,
                           2.0 * xi_x * xi_y, 2.0 * xi_x * xi_z, 2.0 * xi_y * xi_z,
                           0.8 * xi_x * heat_factor, 0.8 * xi_y * heat_factor, 0.8 * xi_z * heat_factor])
    return xi_x, xi_y, xi_z, moment_rows, equilibrium_rows, grad_rows


def relax(padded, held_moments, reaction, gas_cells, coupling):
    upper_x = padded[:, 2:, 1:-1, 1:-1]
    lower_x = padded[:, :-2, 1:-1, 1:-1]
    upper_y = padded[:, 1:-1, 2:, 1:-1]
    lower_y = padded[:, 1:-1, :-2, 1:-1]
    upper_z = padded[:, 1:-1, 1:-1, 2:]
    lower_z = padded[:, 1:-1, 1:-1, :-2]
    beside_all = upper_x + lower_x + upper_y + lower_y + upper_z + lower_z
    coupled = (jnp.einsum('kl,lxyz->kxyz', coupling[0], upper_x - lower_x, precision=lax.Precision.HIGHEST)
               + jnp.einsum('kl,lxyz->kxyz', coupling[1], upper_y - lower_y, precision=lax.Precision.HIGHEST)
               + jnp.einsum('kl,lxyz->kxyz', coupling[2], upper_z - lower_z, precision=lax.Precision.HIGHEST))
    updated = (reaction * held_moments + DIFFUSION * beside_all - 0.5 * coupled) / (reaction + 6.0 * DIFFUSION)
    return jnp.where(gas_cells, updated, held_moments)


def reference(distribution, velocity_order, macro_state, rarefaction, wall_mask):
    is_wall = wall_mask != 0
    moving = (wall_mask == 2).astype(jnp.float32)
    block_size = min(NV, 4096)
    block_count = NV // block_size
    dist_blocks = distribution.reshape(block_count, block_size, NX, NY * NZ)
    order_blocks = velocity_order.reshape(block_count, block_size)
    macro_flat = macro_state.reshape(13, NX * NY * NZ)
    rate_field = rarefaction.reshape(1, NX, NY, NZ)
    wall_field = is_wall.reshape(1, NX, NY, NZ)

    def one_block(block_pair):
        dist_part, order_part = block_pair
        xi_x, xi_y, xi_z, moment_rows, equilibrium_rows, grad_rows = velocity_tables(order_part, NQ)
        wall_state = macro_state[0][None] + 2.0 * LID_SPEED * moving[None] * xi_x[:, None, None]
        current = jnp.where(is_wall[None], wall_state, dist_part).reshape(block_size, NX, NY, NZ)
        padded = jnp.pad(current, ((0, 0), (1, 1), (1, 1), (1, 1)))
        lower_x = padded[:, :-2, 1:-1, 1:-1]
        upper_x = padded[:, 2:, 1:-1, 1:-1]
        lower_y = padded[:, 1:-1, :-2, 1:-1]
        upper_y = padded[:, 1:-1, 2:, 1:-1]
        lower_z = padded[:, 1:-1, 1:-1, :-2]
        upper_z = padded[:, 1:-1, 1:-1, 2:]
        speed_x = xi_x[:, None, None, None]
        speed_y = xi_y[:, None, None, None]
        speed_z = xi_z[:, None, None, None]
        upwind = (jnp.abs(speed_x) * jnp.where(speed_x > 0, lower_x, upper_x)
                  + jnp.abs(speed_y) * jnp.where(speed_y > 0, lower_y, upper_y)
                  + jnp.abs(speed_z) * jnp.where(speed_z > 0, lower_z, upper_z))
        eq_state = jnp.dot(equilibrium_rows.T, macro_flat,
                           precision=lax.Precision.HIGHEST).reshape(block_size, NX, NY, NZ)
        denominator = rate_field + jnp.abs(speed_x) + jnp.abs(speed_y) + jnp.abs(speed_z)
        updated = jnp.where(wall_field, wall_state.reshape(block_size, NX, NY, NZ),
                            (rate_field * eq_state + upwind) / denominator)
        updated = updated.reshape(block_size, NX * NY * NZ)
        partial_value = jnp.dot(moment_rows, updated, precision=lax.Precision.HIGHEST)
        return updated, partial_value

    updated_blocks, partials = lax.map(one_block, (dist_blocks, order_blocks))
    held_moments = jnp.sum(partials, axis=0).reshape(13, NX, NY, NZ)
    reaction = REACTION * (1.0 + rate_field)
    gas_cells = jnp.logical_not(wall_field)
    coupling = coupling_tables(held_moments.dtype)
    moments_now = held_moments
    for sweep_index in range(SWEEPS):
        padded = jnp.pad(moments_now, ((0, 0), (1, 1), (1, 1), (1, 1)))
        moments_now = relax(padded, held_moments, reaction, gas_cells, coupling)
    change = (moments_now - held_moments).reshape(13, NX * NY * NZ)

    def correct_block(block_pair):
        updated_part, order_part = block_pair
        grad_rows = velocity_tables(order_part, NQ)[5]
        return updated_part + jnp.dot(grad_rows.T, change, precision=lax.Precision.HIGHEST)

    dist_out = lax.map(correct_block, (updated_blocks, order_blocks))
    return dist_out.reshape(NV, NX, NY * NZ), moments_now.reshape(13, NX, NY * NZ)
```

```python
import functools
import math

import jax
import jax.numpy as jnp
import numpy as np
from jax import lax
from jax.experimental import pallas as pl
from jax.experimental.pallas import tpu as pltpu
from jax.sharding import PartitionSpec as P

SWEEPS = 4
LID_SPEED = 1.0
COUPLING = (
    (0, 1, 0, 0.24),
    (0, 2, 1, 0.24),
    (0, 3, 2, 0.24),
    (1, 0, 0, 0.2),
    (1, 4, 0, 0.2),
    (1, 5, 0, 0.2),
    (1, 7, 1, 0.1),
    (1, 8, 2, 0.1),
    (2, 0, 1, 0.2),
    (2, 4, 1, 0.2),
    (2, 6, 1, 0.2),
    (2, 7, 0, 0.1),
    (2, 9, 2, 0.1),
    (3, 0, 2, 0.2),
    (3, 4, 2, 0.2),
    (3, 8, 0, 0.1),
    (3, 9, 1, 0.1),
    (4, 10, 0, 0.2),
    (4, 11, 1, 0.2),
    (4, 12, 2, 0.2),
    (5, 1, 0, 0.4),
    (5, 10, 0, 0.2),
    (6, 2, 1, 0.4),
    (6, 11, 1, 0.2),
    (7, 1, 1, 0.2),
    (7, 2, 0, 0.2),
    (8, 1, 2, 0.2),
    (8, 3, 0, 0.2),
    (9, 2, 2, 0.2),
    (9, 3, 1, 0.2),
    (10, 4, 0, 0.5),
    (10, 5, 0, 0.2),
    (11, 4, 1, 0.5),
    (11, 6, 1, 0.2),
    (12, 4, 2, 0.5),
    (12, 8, 0, 0.1),
    (12, 9, 1, 0.1),
)


PLANES = 4
LANES = 128
SHIFT_Y = 8
SHIFT_Z = 1
CHUNK = 256
SUB = 128
COLS = 10
MESH = pl.DeviceIdType.MESH


def coupling_matrix():
    table = np.zeros((16, 48), np.float32)
    for row, column, dim, value in COUPLING:
        table[row, dim * 16 + column] = value
    return table


def split(x):
    high = x.astype(jnp.bfloat16)
    low = (x - high.astype(jnp.float32)).astype(jnp.bfloat16)
    return high, low


def store_rows(ref, rows):
    for k, row in enumerate(rows):
        ref[pl.ds(k, 1), :] = row


def transport_kernel(
    n_space, n_vel, chunks,
    dist_ref, order_ref, macro_ref, rate_ref, wall_ref, coupling_ref,
    upd_ref, grad_ref, change_ref, mom_ref,
    dist, halo, stage, upd, table, eq_t, mom_t, rhs, rhs_f, acc, fields, fields_src,
    rs_src, rs_dst, reduced, held,
    in_sem, out_sem, halo_send, halo_recv, fld_send, fld_recv, rs_send, rs_recv, ag_send, ag_recv,
):
    space = lax.axis_index("space")
    vel = lax.axis_index("vel")
    has_left = space > 0
    has_right = space < n_space - 1
    rows_part = 16 * PLANES // n_vel
    per_plane = n_vel // PLANES

    def in_copy(i):
        rows = pl.ds(i * (CHUNK * PLANES), CHUNK * PLANES)
        return pltpu.make_async_copy(dist_ref.at[rows, :], dist.at[i], in_sem.at[i])

    def load_chunk(c, carry):
        in_copy(c).start()
        in_copy(chunks + c).start()
        return carry

    lax.fori_loop(0, chunks, load_chunk, 0)

    barrier = pltpu.get_barrier_semaphore()
    for off in range(n_vel):
        peer = lax.rem(vel + off, n_vel)
        if off:
            pl.semaphore_signal(barrier, inc=1, device_id={"vel": peer}, device_id_type=MESH)

        @pl.when(has_left)
        def _():
            pl.semaphore_signal(
                barrier, inc=1, device_id={"space": space - 1, "vel": peer}, device_id_type=MESH
            )

        @pl.when(has_right)
        def _():
            pl.semaphore_signal(
                barrier, inc=1, device_id={"space": space + 1, "vel": peer}, device_id_type=MESH
            )

    fields_src[0:4, :] = rate_ref[...]
    fields_src[4:8, :] = wall_ref[...].astype(jnp.float32)
    fields_src[8:12, :] = macro_ref[0]
    fields_src[12:16, :] = jnp.zeros((4, LANES), jnp.float32)

    @pl.when(jnp.logical_not(has_left))
    def _():
        fields[0] = jnp.zeros((16, LANES), jnp.float32)
        held[0] = jnp.zeros(held.shape[1:], jnp.float32)
        halo[0:chunks] = jnp.zeros((chunks, CHUNK, LANES), jnp.float32)

    @pl.when(jnp.logical_not(has_right))
    def _():
        fields[1] = jnp.zeros((16, LANES), jnp.float32)
        held[2] = jnp.zeros(held.shape[1:], jnp.float32)
        halo[chunks : 2 * chunks] = jnp.zeros((chunks, CHUNK, LANES), jnp.float32)

    beside = jnp.minimum(space, 1) + jnp.minimum(n_space - 1 - space, 1)
    pl.semaphore_wait(barrier, n_vel - 1 + n_vel * beside)

    def fields_copy(side):
        return pltpu.make_async_remote_copy(
            fields_src, fields.at[side], fld_send.at[side], fld_recv.at[side],
            device_id={"space": space + 1 if side == 0 else space - 1}, device_id_type=MESH,
        )

    def halo_copy(side, i):
        return pltpu.make_async_remote_copy(
            stage.at[i], halo.at[i], halo_send.at[i], halo_recv.at[i],
            device_id={"space": space + 1 if side == 0 else space - 1}, device_id_type=MESH,
        )

    sends = (has_right, has_left)
    receives = (has_left, has_right)
    for side in range(2):

        @pl.when(sends[side])
        def _():
            fields_copy(side).start()

    def send_halo(c, carry):
        for side in range(2):
            i = side * chunks + c
            in_copy(i).wait()
            plane = PLANES - 1 if side == 0 else 0

            @pl.when(sends[side])
            def _():
                stage[i] = dist[i, pl.ds(plane, CHUNK, stride=PLANES), :]
                halo_copy(side, i).start()

        return carry

    lax.fori_loop(0, chunks, send_halo, 0)

    def make_tables(i, carry):
        order = order_ref[i]
        x = ((order >> 10) * 2 - 31).astype(jnp.float32) * 0.125
        y = (((order >> 5) & 31) * 2 - 31).astype(jnp.float32) * 0.125
        z = ((order & 31) * 2 - 31).astype(jnp.float32) * 0.125
        square = x * x + y * y + z * z
        one = jnp.ones_like(x)
        zero = jnp.zeros_like(x)
        energy = square - 1.5
        heat = square - 2.5
        store_rows(
            table,
            [one, x, y, z, energy, x * heat, y * heat, z * heat,
             jnp.abs(x), jnp.abs(y), jnp.abs(z),
             jnp.where(y > 0, 1.0, -1.0), jnp.where(z > 0, 1.0, -1.0), zero, zero, zero],
        )
        high, low = split(table[...])
        eq_t[i, 0:16, :] = high
        eq_t[i, 16:32, :] = low
        eq_t[i, 32:48, :] = high
        weight = jnp.exp(-square) * (0.25**3 / math.pi**1.5)
        third = square * (1.0 / 3.0)
        store_rows(
            table,
            [weight, weight * x, weight * y, weight * z, weight * energy * (2.0 / 3.0),
             2.0 * weight * (x * x - third), 2.0 * weight * (y * y - third),
             2.0 * weight * (x * y), 2.0 * weight * (x * z), 2.0 * weight * (y * z),
             weight * x * heat, weight * y * heat, weight * z * heat, zero, zero, zero],
        )
        high, low = split(table[...])
        mom_t[i, 0:16, :] = high
        mom_t[i, 16:32, :] = low
        store_rows(
            table,
            [one, 2.0 * x, 2.0 * y, 2.0 * z, energy, x * x - z * z, y * y - z * z,
             2.0 * x * y, 2.0 * x * z, 2.0 * y * z,
             0.8 * x * heat, 0.8 * y * heat, 0.8 * z * heat, zero, zero, zero],
        )
        high, low = split(table[...])
        grad_ref[i, 0:16, :] = high
        grad_ref[i, 16:32, :] = low
        grad_ref[i, 32:48, :] = high
        return carry

    lax.fori_loop(0, 2 * chunks, make_tables, 0)

    zero_row = jnp.zeros((1, LANES), jnp.float32)
    rhs_f[...] = jnp.zeros((16, COLS * LANES), jnp.float32)
    shakhov = 4.0 / 15.0
    for p in range(PLANES):
        rate = rate_ref[pl.ds(p, 1), :]
        wall = wall_ref[pl.ds(p, 1), :]
        gas = wall == 0
        moving = jnp.where(wall == 2, 2.0 * LID_SPEED, 0.0)
        for k, (source, scale) in enumerate(
            ((0, 1.0), (1, 2.0), (2, 2.0), (3, 2.0), (4, 1.0), (10, shakhov), (11, shakhov), (12, shakhov))
        ):
            value = macro_ref[source, pl.ds(p, 1), :]
            other = value if k == 0 else moving if k == 1 else zero_row
            rhs_f[pl.ds(k, 1), pl.ds(p * LANES, LANES)] = jnp.where(gas, rate * value * scale, other)
    lane = lax.broadcasted_iota(jnp.int32, (1, LANES), 1).astype(jnp.float32)
    one_row = jnp.ones((1, LANES), jnp.float32)
    for k in range(3):
        rhs_f[pl.ds(8 + k, 1), pl.ds((5 + k) * LANES, LANES)] = one_row
    for k, step in enumerate((SHIFT_Y, SHIFT_Z)):
        rhs_f[pl.ds(0, 1), pl.ds((8 + k) * LANES, LANES)] = lane
        rhs_f[pl.ds(11 + k, 1), pl.ds((8 + k) * LANES, LANES)] = one_row * (-1.0 * step)

    for side in range(2):

        @pl.when(receives[side])
        def _():
            fields_copy(side).wait_recv()

        plane = PLANES - 1 if side == 0 else 0
        wall_next = fields[side, pl.ds(4 + plane, 1), :]
        rhs_f[pl.ds(0, 1), pl.ds(4 * LANES, LANES)] = fields[side, pl.ds(8 + plane, 1), :]
        rhs_f[pl.ds(1, 1), pl.ds(4 * LANES, LANES)] = jnp.where(wall_next > 1.5, 2.0 * LID_SPEED, 0.0)
        high, low = split(rhs_f[...])
        rhs[side, 0:16, :] = high
        rhs[side, 16:32, :] = high
        rhs[side, 32:48, :] = low

    acc[...] = jnp.zeros(acc.shape, jnp.float32)

    def out_copy(i):
        slots = pl.ds(i * CHUNK, CHUNK)
        return pltpu.make_async_copy(upd.at[i], upd_ref.at[i], out_sem.at[i])

    def advance(side, i):
        @pl.when(receives[side])
        def _():
            halo_copy(side, i).wait_recv()

        for sub in range(CHUNK // SUB):
            first = sub * SUB
            lhs = eq_t[i, :, first : first + SUB]
            out = lax.dot_general(
                lhs, rhs[side], (((0,), (0,)), ((), ())), preferred_element_type=jnp.float32
            )
            cols = [out[:, k * LANES : (k + 1) * LANES] for k in range(COLS)]
            speed_x, speed_y, speed_z = cols[5:8]
            index_y = cols[8].astype(jnp.int32) & (LANES - 1)
            index_z = cols[9].astype(jnp.int32) & (LANES - 1)
            total = speed_x + speed_y + speed_z
            gas = [wall_ref[pl.ds(p, 1), :] == 0 for p in range(PLANES)]
            plane = PLANES - 1 if side == 0 else 0
            gas_next = fields[side, pl.ds(4 + plane, 1), :] == 0.0
            current = [
                jnp.where(gas[p], dist[i, pl.ds(first * PLANES + p, SUB, stride=PLANES), :], cols[p])
                for p in range(PLANES)
            ]
            beyond = jnp.where(gas_next, halo[i, first : first + SUB, :], cols[4])
            line = [beyond] + current[:-1] if side == 0 else current[1:] + [beyond]
            for p in range(PLANES):
                along_y = jnp.take_along_axis(current[p], index_y, axis=1, mode="promise_in_bounds")
                along_z = jnp.take_along_axis(current[p], index_z, axis=1, mode="promise_in_bounds")
                flow = cols[p] + speed_x * line[p] + speed_y * along_y + speed_z * along_z
                below = total + rate_ref[pl.ds(p, 1), :]
                guess = pl.reciprocal(below, approx=True)
                guess = guess * (2.0 - below * guess)
                value = jnp.where(gas[p], flow * guess, cols[p])
                upd[i, p, first : first + SUB, :] = value
                high, low = split(value)
                weights = mom_t[i, :, first : first + SUB]
                acc[:, p * LANES : (p + 1) * LANES] += jnp.dot(
                    jnp.concatenate([weights, weights], axis=1),
                    jnp.concatenate([high, low], axis=0),
                    preferred_element_type=jnp.float32,
                )
        out_copy(i).start()

    def step(c, carry):
        for side in range(2):
            advance(side, side * chunks + c)
        return carry

    lax.fori_loop(0, chunks, step, 0)

    for part in range(n_vel):
        plane, k = part // per_plane, part % per_plane
        first = k * rows_part
        lanes = pl.ds(plane * LANES, LANES)
        rs_src[part] = acc[pl.ds(first, rows_part), lanes] + acc[pl.ds(16 + first, rows_part), lanes]

    def rs_copy(off):
        peer = lax.rem(vel + off, n_vel)
        return pltpu.make_async_remote_copy(
            rs_src.at[peer], rs_dst.at[vel], rs_send.at[off], rs_recv.at[vel],
            device_id={"vel": peer}, device_id_type=MESH,
        )

    def rs_arrival(off):
        peer = lax.rem(vel + off, n_vel)
        return pltpu.make_async_remote_copy(
            rs_src.at[peer], rs_dst.at[peer], rs_send.at[off], rs_recv.at[peer],
            device_id={"vel": peer}, device_id_type=MESH,
        )

    for off in range(1, n_vel):
        rs_copy(off).start()
    rs_dst[vel] = rs_src[vel]
    for off in range(1, n_vel):
        rs_arrival(off).wait_recv()
    whole = rs_dst[0]
    for part in range(1, n_vel):
        whole = whole + rs_dst[part]
    reduced[...] = whole

    def ag_copy(shift, off):
        return pltpu.make_async_remote_copy(
            reduced, held.at[1 - shift, vel],
            ag_send.at[1 + shift, off], ag_recv.at[1 - shift, vel],
            device_id={"space": space + shift, "vel": lax.rem(vel + off, n_vel)}, device_id_type=MESH,
        )

    def ag_arrival(k, off):
        peer = lax.rem(vel + off, n_vel)
        return pltpu.make_async_remote_copy(
            reduced, held.at[k, peer],
            ag_send.at[k, off], ag_recv.at[k, peer],
            device_id={"space": space, "vel": peer}, device_id_type=MESH,
        )

    @pl.when(has_left)
    def _():
        for off in range(n_vel):
            ag_copy(-1, off).start()

    @pl.when(has_right)
    def _():
        for off in range(n_vel):
            ag_copy(1, off).start()

    for off in range(1, n_vel):
        ag_copy(0, off).start()
    held[1, vel] = whole
    for off in range(1, n_vel):
        ag_arrival(1, off).wait_recv()

    @pl.when(has_left)
    def _():
        for off in range(n_vel):
            ag_arrival(0, off).wait_recv()

    @pl.when(has_right)
    def _():
        for off in range(n_vel):
            ag_arrival(2, off).wait_recv()

    start = []
    for k in range(3):
        for p in range(PLANES):
            parts = [held[k, p * per_plane + m] for m in range(per_plane)]
            start.append(parts[0] if per_plane == 1 else jnp.concatenate(parts, axis=0))
    reaction, gas = [], []
    for k in range(3):
        for p in range(PLANES):
            source = fields_src if k == 1 else fields.at[0 if k == 0 else 1]
            reaction.append(1.0 + source[pl.ds(p, 1), :])
            gas.append(source[pl.ds(4 + p, 1), :] == 0.0)
    now = list(start)
    count = len(start)
    for sweep in range(1, SWEEPS + 1):
        inner = range(sweep, count - sweep)
        sums, differences = [], []
        for p in inner:
            up_y = pltpu.roll(now[p], LANES - SHIFT_Y, 1)
            down_y = pltpu.roll(now[p], SHIFT_Y, 1)
            up_z = pltpu.roll(now[p], LANES - SHIFT_Z, 1)
            down_z = pltpu.roll(now[p], SHIFT_Z, 1)
            sums.append(now[p + 1] + now[p - 1] + up_y + down_y + up_z + down_z)
            differences.append(
                jnp.concatenate([now[p + 1] - now[p - 1], up_y - down_y, up_z - down_z], axis=0)
            )
        high, low = split(jnp.concatenate(differences, axis=1))
        coupled = jnp.dot(
            coupling_ref[...],
            jnp.concatenate([high, high, low], axis=0),
            preferred_element_type=jnp.float32,
        )
        later = list(now)
        for m, p in enumerate(inner):
            value = reaction[p] * start[p] + sums[m] - 0.5 * coupled[:, m * LANES : (m + 1) * LANES]
            later[p] = jnp.where(gas[p], value / (reaction[p] + 6.0), start[p])
        now = later

    for p in range(PLANES):
        lanes = pl.ds(p * LANES, LANES)
        high, low = split(now[PLANES + p] - start[PLANES + p])
        change_ref[0:16, lanes] = high
        change_ref[16:32, lanes] = high
        change_ref[32:48, lanes] = low
        for k in range(13):
            mom_ref[k, pl.ds(p, 1), :] = now[PLANES + p][k : k + 1, :]

    def drain(c, carry):
        for side in range(2):
            i = side * chunks + c
            out_copy(i).wait()

            @pl.when(sends[side])
            def _():
                halo_copy(side, i).wait_send()

        return carry

    lax.fori_loop(0, chunks, drain, 0)
    for side in range(2):

        @pl.when(sends[side])
        def _():
            fields_copy(side).wait_send()

    for off in range(1, n_vel):
        rs_copy(off).wait_send()
        ag_copy(0, off).wait_send()

    @pl.when(has_left)
    def _():
        for off in range(n_vel):
            ag_copy(-1, off).wait_send()

    @pl.when(has_right)
    def _():
        for off in range(n_vel):
            ag_copy(1, off).wait_send()


def correct_kernel(group, upd_ref, grad_ref, change_ref, settled_ref, out_ref, mom_ref):
    @pl.when(pl.program_id(0) == 0)
    def _():
        mom_ref[...] = settled_ref[...]

    for i in range(group):
        change = lax.dot_general(
            grad_ref[i], change_ref[...], (((0,), (0,)), ((), ())), preferred_element_type=jnp.float32
        )
        for p in range(PLANES):
            rows = pl.ds(i * CHUNK * PLANES + p, CHUNK, stride=PLANES)
            out_ref[rows, :] = upd_ref[i, p] + change[:, p * LANES : (p + 1) * LANES]


def local(n_space, n_vel, distribution, velocity_order, macro_state, rarefaction, wall_mask):
    slots = distribution.shape[0]
    pieces = slots // CHUNK
    chunks = pieces // 2
    f32, bf16 = jnp.float32, jnp.bfloat16
    table = coupling_matrix()
    high = table.astype(bf16)
    low = (table - high.astype(np.float32)).astype(bf16)
    coupling = jnp.asarray(np.concatenate([high, low, high], axis=1))
    rows_part = 16 * PLANES // n_vel
    vmem = pl.BlockSpec(memory_space=pltpu.VMEM)
    hbm = pl.BlockSpec(memory_space=pl.ANY)
    dma = pltpu.SemaphoreType.DMA
    updated, grad, change, settled = pl.pallas_call(
        functools.partial(transport_kernel, n_space, n_vel, chunks),
        out_shape=(
            jax.ShapeDtypeStruct((pieces, PLANES, CHUNK, LANES), f32),
            jax.ShapeDtypeStruct((pieces, 48, CHUNK), bf16),
            jax.ShapeDtypeStruct((48, PLANES * LANES), bf16),
            jax.ShapeDtypeStruct((13, PLANES, LANES), f32),
        ),
        in_specs=[hbm, vmem, vmem, vmem, vmem, vmem],
        out_specs=(hbm, vmem, vmem, vmem),
        scratch_shapes=[
            pltpu.VMEM((pieces, CHUNK * PLANES, LANES), f32),
            pltpu.VMEM((pieces, CHUNK, LANES), f32),
            pltpu.VMEM((pieces, CHUNK, LANES), f32),
            pltpu.VMEM((pieces, PLANES, CHUNK, LANES), f32),
            pltpu.VMEM((16, CHUNK), f32),
            pltpu.VMEM((pieces, 48, CHUNK), bf16),
            pltpu.VMEM((pieces, 32, CHUNK), bf16),
            pltpu.VMEM((2, 48, COLS * LANES), bf16),
            pltpu.VMEM((16, COLS * LANES), f32),
            pltpu.VMEM((32, PLANES * LANES), f32),
            pltpu.VMEM((2, 16, LANES), f32),
            pltpu.VMEM((16, LANES), f32),
            pltpu.VMEM((n_vel, rows_part, LANES), f32),
            pltpu.VMEM((n_vel, rows_part, LANES), f32),
            pltpu.VMEM((rows_part, LANES), f32),
            pltpu.VMEM((3, n_vel, rows_part, LANES), f32),
            dma((pieces,)), dma((pieces,)), dma((pieces,)), dma((pieces,)),
            dma((2,)), dma((2,)), dma((n_vel,)), dma((n_vel,)), dma((3, n_vel)), dma((3, n_vel)),
        ],
        compiler_params=pltpu.CompilerParams(
            collective_id=0, has_side_effects=True, vmem_limit_bytes=48 * 2**20
        ),
        name="transport",
    )(
        distribution.reshape(slots * PLANES, LANES),
        velocity_order.reshape(pieces, 1, CHUNK),
        macro_state,
        rarefaction,
        wall_mask,
        coupling,
    )
    group = 2
    out, moments = pl.pallas_call(
        functools.partial(correct_kernel, group),
        grid=(pieces // group,),
        out_shape=(
            jax.ShapeDtypeStruct((slots * PLANES, LANES), f32),
            jax.ShapeDtypeStruct((13, PLANES, LANES), f32),
        ),
        in_specs=[
            pl.BlockSpec((group, PLANES, CHUNK, LANES), lambda g: (g, 0, 0, 0)),
            pl.BlockSpec((group, 48, CHUNK), lambda g: (g, 0, 0)),
            pl.BlockSpec((48, PLANES * LANES), lambda g: (0, 0)),
            pl.BlockSpec((13, PLANES, LANES), lambda g: (0, 0, 0)),
        ],
        out_specs=(
            pl.BlockSpec((group * CHUNK * PLANES, LANES), lambda g: (g, 0)),
            pl.BlockSpec((13, PLANES, LANES), lambda g: (0, 0, 0)),
        ),
        compiler_params=pltpu.CompilerParams(vmem_limit_bytes=32 * 2**20),
        name="correct",
    )(updated, grad, change, settled)
    return out.reshape(slots, PLANES, LANES), moments


def solution(mesh):
    return jax.shard_map(
        functools.partial(local, mesh.shape["space"], mesh.shape["vel"]),
        mesh=mesh,
        in_specs=(
            P("vel", "space", None),
            P("vel"),
            P(None, "space", None),
            P("space", None),
            P("space", None),
        ),
        out_specs=(P("vel", "space", None), P(None, "space", None)),
        check_vma=False,
    )
```

```python
import functools
import math

import jax
import jax.numpy as jnp
import numpy as np
from jax import lax
from jax.experimental import pallas as pl
from jax.experimental.pallas import tpu as pltpu
from jax.sharding import PartitionSpec as P

SWEEPS = 4
LID_SPEED = 1.0
COUPLING = (
    (0, 1, 0, 0.24),
    (0, 2, 1, 0.24),
    (0, 3, 2, 0.24),
    (1, 0, 0, 0.2),
    (1, 4, 0, 0.2),
    (1, 5, 0, 0.2),
    (1, 7, 1, 0.1),
    (1, 8, 2, 0.1),
    (2, 0, 1, 0.2),
    (2, 4, 1, 0.2),
    (2, 6, 1, 0.2),
    (2, 7, 0, 0.1),
    (2, 9, 2, 0.1),
    (3, 0, 2, 0.2),
    (3, 4, 2, 0.2),
    (3, 8, 0, 0.1),
    (3, 9, 1, 0.1),
    (4, 10, 0, 0.2),
    (4, 11, 1, 0.2),
    (4, 12, 2, 0.2),
    (5, 1, 0, 0.4),
    (5, 10, 0, 0.2),
    (6, 2, 1, 0.4),
    (6, 11, 1, 0.2),
    (7, 1, 1, 0.2),
    (7, 2, 0, 0.2),
    (8, 1, 2, 0.2),
    (8, 3, 0, 0.2),
    (9, 2, 2, 0.2),
    (9, 3, 1, 0.2),
    (10, 4, 0, 0.5),
    (10, 5, 0, 0.2),
    (11, 4, 1, 0.5),
    (11, 6, 1, 0.2),
    (12, 4, 2, 0.5),
    (12, 8, 0, 0.1),
    (12, 9, 1, 0.1),
)


PLANES = 4
LANES = 128
SHIFT_Y = 8
SHIFT_Z = 1
CHUNK = 256
SUB = 128
COLS = 10
MESH = pl.DeviceIdType.MESH


def split(x):
    high = x.astype(jnp.bfloat16)
    low = (x - high.astype(jnp.float32)).astype(jnp.bfloat16)
    return high, low


def store_rows(ref, rows):
    for k, row in enumerate(rows):
        ref[pl.ds(k, 1), :] = row


def transport_kernel(
    n_space, n_vel, chunks,
    dist_ref, order_hbm, macro_hbm, rate_hbm, wall_hbm,
    upd, grad_ref, change_ref, mom_ref,
    order_ref, macro_ref, rate_ref, wall_ref,
    dist, halo, stage, table, eq_t, mom_t, rhs, rhs_f, acc, fields, fields_src,
    rs_src, rs_dst, reduced, held,
    small_sem, in_sem, halo_send, halo_recv, fld_send, fld_recv, rs_send, rs_recv, ag_send, ag_recv,
):
    space = lax.axis_index("space")
    vel = lax.axis_index("vel")
    has_left = space > 0
    has_right = space < n_space - 1
    rows_part = 16 * PLANES // n_vel
    per_plane = n_vel // PLANES

    small = [
        pltpu.make_async_copy(source, target, small_sem.at[k])
        for k, (source, target) in enumerate(
            (
                (rate_hbm, rate_ref), (wall_hbm, wall_ref), (macro_hbm, macro_ref),
                (order_hbm, order_ref),
            )
        )
    ]
    for copy in small:
        copy.start()

    def in_copy(i):
        rows = pl.ds(i * (CHUNK * PLANES), CHUNK * PLANES)
        return pltpu.make_async_copy(dist_ref.at[rows, :], dist.at[i], in_sem.at[i])

    def load_chunk(c, carry):
        in_copy(c).start()
        in_copy(chunks + c).start()
        return carry

    lax.fori_loop(0, chunks, load_chunk, 0)

    barrier = pltpu.get_barrier_semaphore()
    for off in range(n_vel):
        peer = lax.rem(vel + off, n_vel)
        if off:
            pl.semaphore_signal(barrier, inc=1, device_id={"vel": peer}, device_id_type=MESH)

        @pl.when(has_left)
        def _():
            pl.semaphore_signal(
                barrier, inc=1, device_id={"space": space - 1, "vel": peer}, device_id_type=MESH
            )

        @pl.when(has_right)
        def _():
            pl.semaphore_signal(
                barrier, inc=1, device_id={"space": space + 1, "vel": peer}, device_id_type=MESH
            )

    for copy in small[:3]:
        copy.wait()

    fields_src[0:4, :] = rate_ref[...]
    fields_src[4:8, :] = wall_ref[...].astype(jnp.float32)
    fields_src[8:12, :] = macro_ref[0]
    fields_src[12:16, :] = jnp.zeros((4, LANES), jnp.float32)

    @pl.when(jnp.logical_not(has_left))
    def _():
        fields[0] = jnp.zeros((16, LANES), jnp.float32)
        held[0] = jnp.zeros(held.shape[1:], jnp.float32)
        halo[0:chunks] = jnp.zeros((chunks, CHUNK, LANES), jnp.float32)

    @pl.when(jnp.logical_not(has_right))
    def _():
        fields[1] = jnp.zeros((16, LANES), jnp.float32)
        held[2] = jnp.zeros(held.shape[1:], jnp.float32)
        halo[chunks : 2 * chunks] = jnp.zeros((chunks, CHUNK, LANES), jnp.float32)

    beside = jnp.minimum(space, 1) + jnp.minimum(n_space - 1 - space, 1)
    pl.semaphore_wait(barrier, n_vel - 1 + n_vel * beside)

    def fields_copy(side):
        return pltpu.make_async_remote_copy(
            fields_src, fields.at[side], fld_send.at[side], fld_recv.at[side],
            device_id={"space": space + 1 if side == 0 else space - 1}, device_id_type=MESH,
        )

    def halo_copy(side, i):
        return pltpu.make_async_remote_copy(
            stage.at[i], halo.at[i], halo_send.at[i], halo_recv.at[i],
            device_id={"space": space + 1 if side == 0 else space - 1}, device_id_type=MESH,
        )

    sends = (has_right, has_left)
    receives = (has_left, has_right)
    for side in range(2):

        @pl.when(sends[side])
        def _():
            fields_copy(side).start()

    def send_halo(c, carry):
        for side in range(2):
            i = side * chunks + c
            in_copy(i).wait()
            plane = PLANES - 1 if side == 0 else 0

            @pl.when(sends[side])
            def _():
                stage[i] = dist[i, pl.ds(plane, CHUNK, stride=PLANES), :]
                halo_copy(side, i).start()

        return carry

    lax.fori_loop(0, chunks, send_halo, 0)

    small[3].wait()

    def make_tables(i, carry):
        order = order_ref[i]
        x = ((order >> 10) * 2 - 31).astype(jnp.float32) * 0.125
        y = (((order >> 5) & 31) * 2 - 31).astype(jnp.float32) * 0.125
        z = ((order & 31) * 2 - 31).astype(jnp.float32) * 0.125
        square = x * x + y * y + z * z
        one = jnp.ones_like(x)
        zero = jnp.zeros_like(x)
        energy = square - 1.5
        heat = square - 2.5
        store_rows(
            table,
            [one, x, y, z, energy, x * heat, y * heat, z * heat,
             jnp.abs(x), jnp.abs(y), jnp.abs(z),
             jnp.where(y > 0, 1.0, -1.0), jnp.where(z > 0, 1.0, -1.0), zero, zero, zero],
        )
        high, low = split(table[...])
        eq_t[i, 0:16, :] = high
        eq_t[i, 16:32, :] = low
        eq_t[i, 32:48, :] = high
        weight = jnp.exp(-square) * (0.25**3 / math.pi**1.5)
        third = square * (1.0 / 3.0)
        store_rows(
            table,
            [weight, weight * x, weight * y, weight * z, weight * energy * (2.0 / 3.0),
             2.0 * weight * (x * x - third), 2.0 * weight * (y * y - third),
             2.0 * weight * (x * y), 2.0 * weight * (x * z), 2.0 * weight * (y * z),
             weight * x * heat, weight * y * heat, weight * z * heat, zero, zero, zero],
        )
        high, low = split(table[...])
        mom_t[i, 0:16, :] = high
        mom_t[i, 16:32, :] = low
        store_rows(
            table,
            [one, 2.0 * x, 2.0 * y, 2.0 * z, energy, x * x - z * z, y * y - z * z,
             2.0 * x * y, 2.0 * x * z, 2.0 * y * z,
             0.8 * x * heat, 0.8 * y * heat, 0.8 * z * heat, zero, zero, zero],
        )
        high, low = split(table[...])
        grad_ref[i, 0:16, :] = high
        grad_ref[i, 16:32, :] = low
        grad_ref[i, 32:48, :] = high
        return carry

    lax.fori_loop(0, 2 * chunks, make_tables, 0)

    zero_row = jnp.zeros((1, LANES), jnp.float32)
    rhs_f[...] = jnp.zeros((16, COLS * LANES), jnp.float32)
    shakhov = 4.0 / 15.0
    for p in range(PLANES):
        rate = rate_ref[pl.ds(p, 1), :]
        wall = wall_ref[pl.ds(p, 1), :]
        gas = wall == 0
        moving = jnp.where(wall == 2, 2.0 * LID_SPEED, 0.0)
        for k, (source, scale) in enumerate(
            ((0, 1.0), (1, 2.0), (2, 2.0), (3, 2.0), (4, 1.0), (10, shakhov), (11, shakhov), (12, shakhov))
        ):
            value = macro_ref[source, pl.ds(p, 1), :]
            other = value if k == 0 else moving if k == 1 else zero_row
            rhs_f[pl.ds(k, 1), pl.ds(p * LANES, LANES)] = jnp.where(gas, rate * value * scale, other)
    lane = lax.broadcasted_iota(jnp.int32, (1, LANES), 1).astype(jnp.float32)
    one_row = jnp.ones((1, LANES), jnp.float32)
    for k in range(3):
        rhs_f[pl.ds(8 + k, 1), pl.ds((5 + k) * LANES, LANES)] = one_row
    for k, step in enumerate((SHIFT_Y, SHIFT_Z)):
        rhs_f[pl.ds(0, 1), pl.ds((8 + k) * LANES, LANES)] = lane
        rhs_f[pl.ds(11 + k, 1), pl.ds((8 + k) * LANES, LANES)] = one_row * (-1.0 * step)

    for side in range(2):

        @pl.when(receives[side])
        def _():
            fields_copy(side).wait_recv()

        plane = PLANES - 1 if side == 0 else 0
        wall_next = fields[side, pl.ds(4 + plane, 1), :]
        rhs_f[pl.ds(0, 1), pl.ds(4 * LANES, LANES)] = fields[side, pl.ds(8 + plane, 1), :]
        rhs_f[pl.ds(1, 1), pl.ds(4 * LANES, LANES)] = jnp.where(wall_next > 1.5, 2.0 * LID_SPEED, 0.0)
        high, low = split(rhs_f[...])
        rhs[side, 0:16, :] = high
        rhs[side, 16:32, :] = high
        rhs[side, 32:48, :] = low

    acc[...] = jnp.zeros(acc.shape, jnp.float32)

    def advance(side, i):
        @pl.when(receives[side])
        def _():
            halo_copy(side, i).wait_recv()

        for sub in range(CHUNK // SUB):
            first = sub * SUB
            lhs = eq_t[i, :, first : first + SUB]
            out = lax.dot_general(
                lhs, rhs[side], (((0,), (0,)), ((), ())), preferred_element_type=jnp.float32
            )
            cols = [out[:, k * LANES : (k + 1) * LANES] for k in range(COLS)]
            speed_x, speed_y, speed_z = cols[5:8]
            index_y = cols[8].astype(jnp.int32) & (LANES - 1)
            index_z = cols[9].astype(jnp.int32) & (LANES - 1)
            total = speed_x + speed_y + speed_z
            gas = [wall_ref[pl.ds(p, 1), :] == 0 for p in range(PLANES)]
            plane = PLANES - 1 if side == 0 else 0
            gas_next = fields[side, pl.ds(4 + plane, 1), :] == 0.0
            current = [
                jnp.where(gas[p], dist[i, pl.ds(first * PLANES + p, SUB, stride=PLANES), :], cols[p])
                for p in range(PLANES)
            ]
            beyond = jnp.where(gas_next, halo[i, first : first + SUB, :], cols[4])
            line = [beyond] + current[:-1] if side == 0 else current[1:] + [beyond]
            for p in range(PLANES):
                along_y = jnp.take_along_axis(current[p], index_y, axis=1, mode="promise_in_bounds")
                along_z = jnp.take_along_axis(current[p], index_z, axis=1, mode="promise_in_bounds")
                flow = cols[p] + speed_x * line[p] + speed_y * along_y + speed_z * along_z
                below = total + rate_ref[pl.ds(p, 1), :]
                guess = pl.reciprocal(below, approx=True)
                guess = guess * (2.0 - below * guess)
                value = jnp.where(gas[p], flow * guess, cols[p])
                upd[i, p, first : first + SUB, :] = value
                high, low = split(value)
                weights = mom_t[i, :, first : first + SUB]
                acc[:, p * LANES : (p + 1) * LANES] += jnp.dot(
                    jnp.concatenate([weights, weights], axis=1),
                    jnp.concatenate([high, low], axis=0),
                    preferred_element_type=jnp.float32,
                )

    def step(c, carry):
        for side in range(2):
            advance(side, side * chunks + c)
        return carry

    lax.fori_loop(0, chunks, step, 0)

    for part in range(n_vel):
        plane, k = part // per_plane, part % per_plane
        first = k * rows_part
        lanes = pl.ds(plane * LANES, LANES)
        rs_src[part] = acc[pl.ds(first, rows_part), lanes] + acc[pl.ds(16 + first, rows_part), lanes]

    def rs_copy(off):
        peer = lax.rem(vel + off, n_vel)
        return pltpu.make_async_remote_copy(
            rs_src.at[peer], rs_dst.at[vel], rs_send.at[off], rs_recv.at[vel],
            device_id={"vel": peer}, device_id_type=MESH,
        )

    def rs_arrival(off):
        peer = lax.rem(vel + off, n_vel)
        return pltpu.make_async_remote_copy(
            rs_src.at[peer], rs_dst.at[peer], rs_send.at[off], rs_recv.at[peer],
            device_id={"vel": peer}, device_id_type=MESH,
        )

    for off in range(1, n_vel):
        rs_copy(off).start()
    rs_dst[vel] = rs_src[vel]
    for off in range(1, n_vel):
        rs_arrival(off).wait_recv()
    whole = rs_dst[0]
    for part in range(1, n_vel):
        whole = whole + rs_dst[part]
    reduced[...] = whole

    def ag_copy(shift, off):
        return pltpu.make_async_remote_copy(
            reduced, held.at[1 - shift, vel],
            ag_send.at[1 + shift, off], ag_recv.at[1 - shift, vel],
            device_id={"space": space + shift, "vel": lax.rem(vel + off, n_vel)}, device_id_type=MESH,
        )

    def ag_arrival(k, off):
        peer = lax.rem(vel + off, n_vel)
        return pltpu.make_async_remote_copy(
            reduced, held.at[k, peer],
            ag_send.at[k, off], ag_recv.at[k, peer],
            device_id={"space": space, "vel": peer}, device_id_type=MESH,
        )

    @pl.when(has_left)
    def _():
        for off in range(n_vel):
            ag_copy(-1, off).start()

    @pl.when(has_right)
    def _():
        for off in range(n_vel):
            ag_copy(1, off).start()

    for off in range(1, n_vel):
        ag_copy(0, off).start()
    held[1, vel] = whole
    for off in range(1, n_vel):
        ag_arrival(1, off).wait_recv()

    @pl.when(has_left)
    def _():
        for off in range(n_vel):
            ag_arrival(0, off).wait_recv()

    @pl.when(has_right)
    def _():
        for off in range(n_vel):
            ag_arrival(2, off).wait_recv()

    start = []
    for k in range(3):
        for p in range(PLANES):
            parts = [held[k, p * per_plane + m] for m in range(per_plane)]
            start.append(parts[0] if per_plane == 1 else jnp.concatenate(parts, axis=0))
    reaction, gas = [], []
    for k in range(3):
        for p in range(PLANES):
            source = fields_src if k == 1 else fields.at[0 if k == 0 else 1]
            reaction.append(1.0 + source[pl.ds(p, 1), :])
            gas.append(source[pl.ds(4 + p, 1), :] == 0.0)
    now = list(start)
    row = lax.broadcasted_iota(jnp.int32, (16, 48), 0)
    column = lax.broadcasted_iota(jnp.int32, (16, 48), 1)
    weight = jnp.zeros((16, 48), jnp.float32)
    for into, source, dim, value in COUPLING:
        weight = jnp.where((row == into) & (column == dim * 16 + source), value, weight)
    high, low = split(weight)
    coupling = jnp.concatenate([high, low, high], axis=1)
    count = len(start)
    for sweep in range(1, SWEEPS + 1):
        inner = range(sweep, count - sweep)
        sums, differences = [], []
        for p in inner:
            up_y = pltpu.roll(now[p], LANES - SHIFT_Y, 1)
            down_y = pltpu.roll(now[p], SHIFT_Y, 1)
            up_z = pltpu.roll(now[p], LANES - SHIFT_Z, 1)
            down_z = pltpu.roll(now[p], SHIFT_Z, 1)
            sums.append(now[p + 1] + now[p - 1] + up_y + down_y + up_z + down_z)
            differences.append(
                jnp.concatenate([now[p + 1] - now[p - 1], up_y - down_y, up_z - down_z], axis=0)
            )
        high, low = split(jnp.concatenate(differences, axis=1))
        coupled = jnp.dot(
            coupling,
            jnp.concatenate([high, high, low], axis=0),
            preferred_element_type=jnp.float32,
        )
        later = list(now)
        for m, p in enumerate(inner):
            value = reaction[p] * start[p] + sums[m] - 0.5 * coupled[:, m * LANES : (m + 1) * LANES]
            later[p] = jnp.where(gas[p], value / (reaction[p] + 6.0), start[p])
        now = later

    for p in range(PLANES):
        lanes = pl.ds(p * LANES, LANES)
        high, low = split(now[PLANES + p] - start[PLANES + p])
        change_ref[0:16, lanes] = high
        change_ref[16:32, lanes] = high
        change_ref[32:48, lanes] = low
        for k in range(13):
            mom_ref[k, pl.ds(p, 1), :] = now[PLANES + p][k : k + 1, :]

    def drain(c, carry):
        for side in range(2):
            i = side * chunks + c
            @pl.when(sends[side])
            def _():
                halo_copy(side, i).wait_send()

        return carry

    lax.fori_loop(0, chunks, drain, 0)
    for side in range(2):

        @pl.when(sends[side])
        def _():
            fields_copy(side).wait_send()

    for off in range(1, n_vel):
        rs_copy(off).wait_send()
        ag_copy(0, off).wait_send()

    @pl.when(has_left)
    def _():
        for off in range(n_vel):
            ag_copy(-1, off).wait_send()

    @pl.when(has_right)
    def _():
        for off in range(n_vel):
            ag_copy(1, off).wait_send()


def correct_kernel(group, upd_ref, grad_ref, change_ref, settled_ref, out_ref, mom_ref):
    @pl.when(pl.program_id(0) == 0)
    def _():
        mom_ref[...] = settled_ref[...]

    base = pl.program_id(0) * group
    for i in range(group):
        change = lax.dot_general(
            grad_ref[base + i], change_ref[...], (((0,), (0,)), ((), ())), preferred_element_type=jnp.float32
        )
        for p in range(PLANES):
            rows = pl.ds(i * CHUNK * PLANES + p, CHUNK, stride=PLANES)
            out_ref[rows, :] = upd_ref[base + i, p] + change[:, p * LANES : (p + 1) * LANES]


def local(n_space, n_vel, distribution, velocity_order, macro_state, rarefaction, wall_mask):
    slots = distribution.shape[0]
    pieces = slots // CHUNK
    chunks = pieces // 2
    f32, bf16 = jnp.float32, jnp.bfloat16
    rows_part = 16 * PLANES // n_vel
    vmem = pl.BlockSpec(memory_space=pltpu.VMEM)
    hbm = pl.BlockSpec(memory_space=pltpu.HBM)
    dma = pltpu.SemaphoreType.DMA
    updated, grad, change, settled = pl.pallas_call(
        functools.partial(transport_kernel, n_space, n_vel, chunks),
        out_shape=(
            jax.ShapeDtypeStruct((pieces, PLANES, CHUNK, LANES), f32),
            jax.ShapeDtypeStruct((pieces, 48, CHUNK), bf16),
            jax.ShapeDtypeStruct((48, PLANES * LANES), bf16),
            jax.ShapeDtypeStruct((13, PLANES, LANES), f32),
        ),
        in_specs=[hbm] * 5,
        out_specs=(vmem,) * 4,
        scratch_shapes=[
            pltpu.VMEM((pieces, 1, CHUNK), jnp.int32),
            pltpu.VMEM((13, PLANES, LANES), f32),
            pltpu.VMEM((PLANES, LANES), f32),
            pltpu.VMEM((PLANES, LANES), jnp.int32),
            pltpu.VMEM((pieces, CHUNK * PLANES, LANES), f32),
            pltpu.VMEM((pieces, CHUNK, LANES), f32),
            pltpu.VMEM((pieces, CHUNK, LANES), f32),
            pltpu.VMEM((16, CHUNK), f32),
            pltpu.VMEM((pieces, 48, CHUNK), bf16),
            pltpu.VMEM((pieces, 32, CHUNK), bf16),
            pltpu.VMEM((2, 48, COLS * LANES), bf16),
            pltpu.VMEM((16, COLS * LANES), f32),
            pltpu.VMEM((32, PLANES * LANES), f32),
            pltpu.VMEM((2, 16, LANES), f32),
            pltpu.VMEM((16, LANES), f32),
            pltpu.VMEM((n_vel, rows_part, LANES), f32),
            pltpu.VMEM((n_vel, rows_part, LANES), f32),
            pltpu.VMEM((rows_part, LANES), f32),
            pltpu.VMEM((3, n_vel, rows_part, LANES), f32),
            dma((4,)), dma((pieces,)), dma((pieces,)), dma((pieces,)),
            dma((2,)), dma((2,)), dma((n_vel,)), dma((n_vel,)), dma((3, n_vel)), dma((3, n_vel)),
        ],
        compiler_params=pltpu.CompilerParams(
            collective_id=0, has_side_effects=True, vmem_limit_bytes=40 * 2**20
        ),
        name="transport",
    )(
        distribution.reshape(slots * PLANES, LANES),
        velocity_order.reshape(pieces, 1, CHUNK),
        macro_state,
        rarefaction,
        wall_mask,
    )
    group = 2
    out, moments = pl.pallas_call(
        functools.partial(correct_kernel, group),
        grid=(pieces // group,),
        out_shape=(
            jax.ShapeDtypeStruct((slots * PLANES, LANES), f32),
            jax.ShapeDtypeStruct((13, PLANES, LANES), f32),
        ),
        in_specs=[
            vmem, vmem, vmem, vmem,
        ],
        out_specs=(
            pl.BlockSpec((group * CHUNK * PLANES, LANES), lambda g: (g, 0)),
            pl.BlockSpec((13, PLANES, LANES), lambda g: (0, 0, 0)),
        ),
        compiler_params=pltpu.CompilerParams(vmem_limit_bytes=32 * 2**20),
        name="correct",
    )(updated, grad, change, settled)
    return out.reshape(slots, PLANES, LANES), moments


def solution(mesh):
    return jax.shard_map(
        functools.partial(local, mesh.shape["space"], mesh.shape["vel"]),
        mesh=mesh,
        in_specs=(
            P("vel", "space", None),
            P("vel"),
            P(None, "space", None),
            P("space", None),
            P("space", None),
        ),
        out_specs=(P("vel", "space", None), P(None, "space", None)),
        check_vma=False,
    )
```

```python
import functools
import math

import jax
import jax.numpy as jnp
import numpy as np
from jax import lax
from jax.experimental import pallas as pl
from jax.experimental.pallas import tpu as pltpu
from jax.sharding import PartitionSpec as P

SWEEPS = 4
LID_SPEED = 1.0
COUPLING = (
    (0, 1, 0, 0.24),
    (0, 2, 1, 0.24),
    (0, 3, 2, 0.24),
    (1, 0, 0, 0.2),
    (1, 4, 0, 0.2),
    (1, 5, 0, 0.2),
    (1, 7, 1, 0.1),
    (1, 8, 2, 0.1),
    (2, 0, 1, 0.2),
    (2, 4, 1, 0.2),
    (2, 6, 1, 0.2),
    (2, 7, 0, 0.1),
    (2, 9, 2, 0.1),
    (3, 0, 2, 0.2),
    (3, 4, 2, 0.2),
    (3, 8, 0, 0.1),
    (3, 9, 1, 0.1),
    (4, 10, 0, 0.2),
    (4, 11, 1, 0.2),
    (4, 12, 2, 0.2),
    (5, 1, 0, 0.4),
    (5, 10, 0, 0.2),
    (6, 2, 1, 0.4),
    (6, 11, 1, 0.2),
    (7, 1, 1, 0.2),
    (7, 2, 0, 0.2),
    (8, 1, 2, 0.2),
    (8, 3, 0, 0.2),
    (9, 2, 2, 0.2),
    (9, 3, 1, 0.2),
    (10, 4, 0, 0.5),
    (10, 5, 0, 0.2),
    (11, 4, 1, 0.5),
    (11, 6, 1, 0.2),
    (12, 4, 2, 0.5),
    (12, 8, 0, 0.1),
    (12, 9, 1, 0.1),
)


PLANES = 4
LANES = 128
SHIFT_Y = 8
SHIFT_Z = 1
CHUNK = 256
SUB = 256
COLS = 8
MESH = pl.DeviceIdType.MESH


def in_hbm(x):
    return pltpu.with_memory_space_constraint(x, pltpu.HBM)


def split(x):
    high = x.astype(jnp.bfloat16)
    low = (x - high.astype(jnp.float32)).astype(jnp.bfloat16)
    return high, low


def store_rows(ref, rows):
    for k, row in enumerate(rows):
        ref[pl.ds(k, 1), :] = row


def transport_kernel(
    n_space, n_vel, chunks,
    dist_ref, order_hbm, macro_hbm, rate_hbm, wall_hbm,
    upd, grad_ref, change_ref, mom_ref,
    order_ref, macro_ref, rate_ref, wall_ref,
    dist, halo, stage, table, eq_t, mom_t, rhs, rhs_f, acc, fields, fields_src,
    rs_src, rs_dst, reduced, held,
    small_sem, in_sem, halo_send, halo_recv, fld_send, fld_recv, rs_send, rs_recv, ag_send, ag_recv,
):
    space = lax.axis_index("space")
    vel = lax.axis_index("vel")
    has_left = space > 0
    has_right = space < n_space - 1
    rows_part = 16 * PLANES // n_vel
    per_plane = n_vel // PLANES

    small = [
        pltpu.make_async_copy(source, target, small_sem.at[k])
        for k, (source, target) in enumerate(
            (
                (rate_hbm, rate_ref), (wall_hbm, wall_ref), (macro_hbm, macro_ref),
                (order_hbm, order_ref),
            )
        )
    ]
    for copy in small:
        copy.start()

    def in_copy(i):
        rows = pl.ds(i * (CHUNK * PLANES), CHUNK * PLANES)
        return pltpu.make_async_copy(dist_ref.at[rows, :], dist.at[i], in_sem.at[i])

    def load_chunk(c, carry):
        in_copy(c).start()
        in_copy(chunks + c).start()
        return carry

    lax.fori_loop(0, chunks, load_chunk, 0)

    barrier = pltpu.get_barrier_semaphore()
    for off in range(n_vel):
        peer = lax.rem(vel + off, n_vel)
        if off:
            pl.semaphore_signal(barrier, inc=1, device_id={"vel": peer}, device_id_type=MESH)

        @pl.when(has_left)
        def _():
            pl.semaphore_signal(
                barrier, inc=1, device_id={"space": space - 1, "vel": peer}, device_id_type=MESH
            )

        @pl.when(has_right)
        def _():
            pl.semaphore_signal(
                barrier, inc=1, device_id={"space": space + 1, "vel": peer}, device_id_type=MESH
            )

    for copy in small[:3]:
        copy.wait()

    fields_src[0:4, :] = rate_ref[...]
    fields_src[4:8, :] = wall_ref[...].astype(jnp.float32)
    fields_src[8:12, :] = macro_ref[0]
    fields_src[12:16, :] = jnp.zeros((4, LANES), jnp.float32)

    @pl.when(jnp.logical_not(has_left))
    def _():
        fields[0] = jnp.zeros((16, LANES), jnp.float32)
        held[0] = jnp.zeros(held.shape[1:], jnp.float32)
        halo[0:chunks] = jnp.zeros((chunks, CHUNK, LANES), jnp.float32)

    @pl.when(jnp.logical_not(has_right))
    def _():
        fields[1] = jnp.zeros((16, LANES), jnp.float32)
        held[2] = jnp.zeros(held.shape[1:], jnp.float32)
        halo[chunks : 2 * chunks] = jnp.zeros((chunks, CHUNK, LANES), jnp.float32)

    beside = jnp.minimum(space, 1) + jnp.minimum(n_space - 1 - space, 1)
    pl.semaphore_wait(barrier, n_vel - 1 + n_vel * beside)

    def fields_copy(side):
        return pltpu.make_async_remote_copy(
            fields_src, fields.at[side], fld_send.at[side], fld_recv.at[side],
            device_id={"space": space + 1 if side == 0 else space - 1}, device_id_type=MESH,
        )

    def halo_copy(side, i):
        return pltpu.make_async_remote_copy(
            stage.at[i], halo.at[i], halo_send.at[i], halo_recv.at[i],
            device_id={"space": space + 1 if side == 0 else space - 1}, device_id_type=MESH,
        )

    sends = (has_right, has_left)
    receives = (has_left, has_right)
    for side in range(2):

        @pl.when(sends[side])
        def _():
            fields_copy(side).start()

    def send_halo(c, carry):
        for side in range(2):
            i = side * chunks + c
            in_copy(i).wait()
            plane = PLANES - 1 if side == 0 else 0

            @pl.when(sends[side])
            def _():
                stage[i] = dist[i, pl.ds(plane, CHUNK, stride=PLANES), :]
                halo_copy(side, i).start()

        return carry

    lax.fori_loop(0, chunks, send_halo, 0)

    small[3].wait()

    def make_tables(i, carry):
        order = order_ref[i]
        x = ((order >> 10) * 2 - 31).astype(jnp.float32) * 0.125
        y = (((order >> 5) & 31) * 2 - 31).astype(jnp.float32) * 0.125
        z = ((order & 31) * 2 - 31).astype(jnp.float32) * 0.125
        square = x * x + y * y + z * z
        one = jnp.ones_like(x)
        zero = jnp.zeros_like(x)
        energy = square - 1.5
        heat = square - 2.5
        store_rows(
            table,
            [one, x, y, z, energy, x * heat, y * heat, z * heat,
             zero, zero, zero, zero, zero, zero, zero, zero],
        )
        high, low = split(table[...])
        eq_t[i, 0:16, :] = high
        eq_t[i, 16:32, :] = low
        eq_t[i, 32:48, :] = high
        weight = jnp.exp(-square) * (0.25**3 / math.pi**1.5)
        third = square * (1.0 / 3.0)
        store_rows(
            table,
            [weight, weight * x, weight * y, weight * z, weight * energy * (2.0 / 3.0),
             2.0 * weight * (x * x - third), 2.0 * weight * (y * y - third),
             2.0 * weight * (x * y), 2.0 * weight * (x * z), 2.0 * weight * (y * z),
             weight * x * heat, weight * y * heat, weight * z * heat, zero, zero, zero],
        )
        high, low = split(table[...])
        mom_t[i, 0:16, :] = high
        mom_t[i, 16:32, :] = low
        store_rows(
            table,
            [one, 2.0 * x, 2.0 * y, 2.0 * z, energy, x * x - z * z, y * y - z * z,
             2.0 * x * y, 2.0 * x * z, 2.0 * y * z,
             0.8 * x * heat, 0.8 * y * heat, 0.8 * z * heat, zero, zero, zero],
        )
        high, low = split(table[...])
        grad_ref[i, 0:16, :] = high
        grad_ref[i, 16:32, :] = low
        grad_ref[i, 32:48, :] = high
        return carry

    lax.fori_loop(0, 2 * chunks, make_tables, 0)

    zero_row = jnp.zeros((1, LANES), jnp.float32)
    rhs_f[...] = jnp.zeros((16, COLS * LANES), jnp.float32)
    shakhov = 4.0 / 15.0
    for p in range(PLANES):
        rate = rate_ref[pl.ds(p, 1), :]
        wall = wall_ref[pl.ds(p, 1), :]
        gas = wall == 0
        moving = jnp.where(wall == 2, 2.0 * LID_SPEED, 0.0)
        for k, (source, scale) in enumerate(
            ((0, 1.0), (1, 2.0), (2, 2.0), (3, 2.0), (4, 1.0), (10, shakhov), (11, shakhov), (12, shakhov))
        ):
            value = macro_ref[source, pl.ds(p, 1), :]
            other = value if k == 0 else moving if k == 1 else zero_row
            rhs_f[pl.ds(k, 1), pl.ds(p * LANES, LANES)] = jnp.where(gas, rate * value * scale, other)
    for k in range(3):
        rhs_f[pl.ds(1 + k, 1), pl.ds((5 + k) * LANES, LANES)] = jnp.ones((1, LANES), jnp.float32)

    for side in range(2):

        @pl.when(receives[side])
        def _():
            fields_copy(side).wait_recv()

        plane = PLANES - 1 if side == 0 else 0
        wall_next = fields[side, pl.ds(4 + plane, 1), :]
        rhs_f[pl.ds(0, 1), pl.ds(4 * LANES, LANES)] = fields[side, pl.ds(8 + plane, 1), :]
        rhs_f[pl.ds(1, 1), pl.ds(4 * LANES, LANES)] = jnp.where(wall_next > 1.5, 2.0 * LID_SPEED, 0.0)
        high, low = split(rhs_f[...])
        rhs[side, 0:16, :] = high
        rhs[side, 16:32, :] = high
        rhs[side, 32:48, :] = low

    acc[...] = jnp.zeros(acc.shape, jnp.float32)

    def advance(side, i):
        @pl.when(receives[side])
        def _():
            halo_copy(side, i).wait_recv()

        for sub in range(CHUNK // SUB):
            first = sub * SUB
            lhs = eq_t[i, :, first : first + SUB]
            out = lax.dot_general(
                lhs, rhs[side], (((0,), (0,)), ((), ())), preferred_element_type=jnp.float32
            )
            cols = [out[:, k * LANES : (k + 1) * LANES] for k in range(COLS)]
            speed_x, speed_y, speed_z = (jnp.abs(col) for col in cols[5:8])
            up_y, up_z = cols[6] > 0, cols[7] > 0
            total = speed_x + speed_y + speed_z
            gas = [wall_ref[pl.ds(p, 1), :] == 0 for p in range(PLANES)]
            plane = PLANES - 1 if side == 0 else 0
            gas_next = fields[side, pl.ds(4 + plane, 1), :] == 0.0
            current = [
                jnp.where(gas[p], dist[i, pl.ds(first * PLANES + p, SUB, stride=PLANES), :], cols[p])
                for p in range(PLANES)
            ]
            beyond = jnp.where(gas_next, halo[i, first : first + SUB, :], cols[4])
            line = [beyond] + current[:-1] if side == 0 else current[1:] + [beyond]
            for p in range(PLANES):
                cells = current[p]
                along_y = jnp.where(
                    up_y, pltpu.roll(cells, SHIFT_Y, 1), pltpu.roll(cells, LANES - SHIFT_Y, 1)
                )
                along_z = jnp.where(
                    up_z, pltpu.roll(cells, SHIFT_Z, 1), pltpu.roll(cells, LANES - SHIFT_Z, 1)
                )
                flow = cols[p] + speed_x * line[p] + speed_y * along_y + speed_z * along_z
                below = total + rate_ref[pl.ds(p, 1), :]
                guess = pl.reciprocal(below, approx=True)
                guess = guess * (2.0 - below * guess)
                value = jnp.where(gas[p], flow * guess, cols[p])
                upd[i, p, first : first + SUB, :] = value
                high, low = split(value)
                acc[:, 2 * p * LANES : 2 * (p + 1) * LANES] += jnp.dot(
                    mom_t[i, :, first : first + SUB],
                    jnp.concatenate([high, low], axis=1),
                    preferred_element_type=jnp.float32,
                )

    def step(c, carry):
        for side in range(2):
            advance(side, side * chunks + c)
        return carry

    lax.fori_loop(0, chunks, step, 0)

    for part in range(n_vel):
        plane, k = part // per_plane, part % per_plane
        first = k * rows_part
        tops, lows = pl.ds(first, rows_part), pl.ds(16 + first, rows_part)
        high, low = pl.ds(2 * plane * LANES, LANES), pl.ds((2 * plane + 1) * LANES, LANES)
        rs_src[part] = (acc[tops, high] + acc[tops, low]) + (acc[lows, high] + acc[lows, low])

    def rs_copy(off):
        peer = lax.rem(vel + off, n_vel)
        return pltpu.make_async_remote_copy(
            rs_src.at[peer], rs_dst.at[vel], rs_send.at[off], rs_recv.at[vel],
            device_id={"vel": peer}, device_id_type=MESH,
        )

    def rs_arrival(off):
        peer = lax.rem(vel + off, n_vel)
        return pltpu.make_async_remote_copy(
            rs_src.at[peer], rs_dst.at[peer], rs_send.at[off], rs_recv.at[peer],
            device_id={"vel": peer}, device_id_type=MESH,
        )

    for off in range(1, n_vel):
        rs_copy(off).start()
    rs_dst[vel] = rs_src[vel]
    for off in range(1, n_vel):
        rs_arrival(off).wait_recv()
    whole = rs_dst[0]
    for part in range(1, n_vel):
        whole = whole + rs_dst[part]
    reduced[...] = whole

    def ag_copy(shift, off):
        return pltpu.make_async_remote_copy(
            reduced, held.at[1 - shift, vel],
            ag_send.at[1 + shift, off], ag_recv.at[1 - shift, vel],
            device_id={"space": space + shift, "vel": lax.rem(vel + off, n_vel)}, device_id_type=MESH,
        )

    def ag_arrival(k, off):
        peer = lax.rem(vel + off, n_vel)
        return pltpu.make_async_remote_copy(
            reduced, held.at[k, peer],
            ag_send.at[k, off], ag_recv.at[k, peer],
            device_id={"space": space, "vel": peer}, device_id_type=MESH,
        )

    @pl.when(has_left)
    def _():
        for off in range(n_vel):
            ag_copy(-1, off).start()

    @pl.when(has_right)
    def _():
        for off in range(n_vel):
            ag_copy(1, off).start()

    for off in range(1, n_vel):
        ag_copy(0, off).start()
    held[1, vel] = whole
    for off in range(1, n_vel):
        ag_arrival(1, off).wait_recv()

    @pl.when(has_left)
    def _():
        for off in range(n_vel):
            ag_arrival(0, off).wait_recv()

    @pl.when(has_right)
    def _():
        for off in range(n_vel):
            ag_arrival(2, off).wait_recv()

    start = []
    for k in range(3):
        for p in range(PLANES):
            parts = [held[k, p * per_plane + m] for m in range(per_plane)]
            start.append(parts[0] if per_plane == 1 else jnp.concatenate(parts, axis=0))
    reaction, gas = [], []
    for k in range(3):
        for p in range(PLANES):
            source = fields_src if k == 1 else fields.at[0 if k == 0 else 1]
            reaction.append(1.0 + source[pl.ds(p, 1), :])
            gas.append(source[pl.ds(4 + p, 1), :] == 0.0)
    now = list(start)
    row = lax.broadcasted_iota(jnp.int32, (16, 48), 0)
    column = lax.broadcasted_iota(jnp.int32, (16, 48), 1)
    weight = jnp.zeros((16, 48), jnp.float32)
    for into, source, dim, value in COUPLING:
        weight = jnp.where((row == into) & (column == dim * 16 + source), value, weight)
    high, low = split(weight)
    coupling = jnp.concatenate([high, low, high], axis=1)
    count = len(start)
    for sweep in range(1, SWEEPS + 1):
        inner = range(sweep, count - sweep)
        sums, differences = [], []
        for p in inner:
            up_y = pltpu.roll(now[p], LANES - SHIFT_Y, 1)
            down_y = pltpu.roll(now[p], SHIFT_Y, 1)
            up_z = pltpu.roll(now[p], LANES - SHIFT_Z, 1)
            down_z = pltpu.roll(now[p], SHIFT_Z, 1)
            sums.append(now[p + 1] + now[p - 1] + up_y + down_y + up_z + down_z)
            differences.append(
                jnp.concatenate([now[p + 1] - now[p - 1], up_y - down_y, up_z - down_z], axis=0)
            )
        high, low = split(jnp.concatenate(differences, axis=1))
        coupled = jnp.dot(
            coupling,
            jnp.concatenate([high, high, low], axis=0),
            preferred_element_type=jnp.float32,
        )
        later = list(now)
        for m, p in enumerate(inner):
            value = reaction[p] * start[p] + sums[m] - 0.5 * coupled[:, m * LANES : (m + 1) * LANES]
            later[p] = jnp.where(gas[p], value / (reaction[p] + 6.0), start[p])
        now = later

    for p in range(PLANES):
        lanes = pl.ds(p * LANES, LANES)
        high, low = split(now[PLANES + p] - start[PLANES + p])
        change_ref[0:16, lanes] = high
        change_ref[16:32, lanes] = high
        change_ref[32:48, lanes] = low
        for k in range(13):
            mom_ref[k, pl.ds(p, 1), :] = now[PLANES + p][k : k + 1, :]

    def drain(c, carry):
        for side in range(2):
            i = side * chunks + c
            @pl.when(sends[side])
            def _():
                halo_copy(side, i).wait_send()

        return carry

    lax.fori_loop(0, chunks, drain, 0)
    for side in range(2):

        @pl.when(sends[side])
        def _():
            fields_copy(side).wait_send()

    for off in range(1, n_vel):
        rs_copy(off).wait_send()
        ag_copy(0, off).wait_send()

    @pl.when(has_left)
    def _():
        for off in range(n_vel):
            ag_copy(-1, off).wait_send()

    @pl.when(has_right)
    def _():
        for off in range(n_vel):
            ag_copy(1, off).wait_send()


def correct_kernel(group, upd_ref, grad_ref, change_ref, settled_ref, out_ref, mom_ref):
    @pl.when(pl.program_id(0) == 0)
    def _():
        mom_ref[...] = settled_ref[...]

    base = pl.program_id(0) * group
    for i in range(group):
        change = lax.dot_general(
            grad_ref[base + i], change_ref[...], (((0,), (0,)), ((), ())), preferred_element_type=jnp.float32
        )
        for p in range(PLANES):
            rows = pl.ds(i * CHUNK * PLANES + p, CHUNK, stride=PLANES)
            out_ref[rows, :] = upd_ref[base + i, p] + change[:, p * LANES : (p + 1) * LANES]


def local(n_space, n_vel, distribution, velocity_order, macro_state, rarefaction, wall_mask):
    slots = distribution.shape[0]
    pieces = slots // CHUNK
    chunks = pieces // 2
    f32, bf16 = jnp.float32, jnp.bfloat16
    rows_part = 16 * PLANES // n_vel
    vmem = pl.BlockSpec(memory_space=pltpu.VMEM)
    hbm = pl.BlockSpec(memory_space=pltpu.HBM)
    dma = pltpu.SemaphoreType.DMA
    updated, grad, change, settled = pl.pallas_call(
        functools.partial(transport_kernel, n_space, n_vel, chunks),
        out_shape=(
            jax.ShapeDtypeStruct((pieces, PLANES, CHUNK, LANES), f32),
            jax.ShapeDtypeStruct((pieces, 48, CHUNK), bf16),
            jax.ShapeDtypeStruct((48, PLANES * LANES), bf16),
            jax.ShapeDtypeStruct((13, PLANES, LANES), f32),
        ),
        in_specs=[hbm] * 5,
        out_specs=(vmem,) * 4,
        scratch_shapes=[
            pltpu.VMEM((pieces, 1, CHUNK), jnp.int32),
            pltpu.VMEM((13, PLANES, LANES), f32),
            pltpu.VMEM((PLANES, LANES), f32),
            pltpu.VMEM((PLANES, LANES), jnp.int32),
            pltpu.VMEM((pieces, CHUNK * PLANES, LANES), f32),
            pltpu.VMEM((pieces, CHUNK, LANES), f32),
            pltpu.VMEM((pieces, CHUNK, LANES), f32),
            pltpu.VMEM((16, CHUNK), f32),
            pltpu.VMEM((pieces, 48, CHUNK), bf16),
            pltpu.VMEM((pieces, 32, CHUNK), bf16),
            pltpu.VMEM((2, 48, COLS * LANES), bf16),
            pltpu.VMEM((16, COLS * LANES), f32),
            pltpu.VMEM((32, 2 * PLANES * LANES), f32),
            pltpu.VMEM((2, 16, LANES), f32),
            pltpu.VMEM((16, LANES), f32),
            pltpu.VMEM((n_vel, rows_part, LANES), f32),
            pltpu.VMEM((n_vel, rows_part, LANES), f32),
            pltpu.VMEM((rows_part, LANES), f32),
            pltpu.VMEM((3, n_vel, rows_part, LANES), f32),
            dma((4,)), dma((pieces,)), dma((pieces,)), dma((pieces,)),
            dma((2,)), dma((2,)), dma((n_vel,)), dma((n_vel,)), dma((3, n_vel)), dma((3, n_vel)),
        ],
        compiler_params=pltpu.CompilerParams(
            collective_id=0, has_side_effects=True, vmem_limit_bytes=40 * 2**20
        ),
        name="transport",
    )(
        distribution.reshape(slots * PLANES, LANES),
        in_hbm(velocity_order.reshape(pieces, 1, CHUNK)),
        in_hbm(macro_state),
        in_hbm(rarefaction),
        in_hbm(wall_mask),
    )
    group = 4
    out, moments = pl.pallas_call(
        functools.partial(correct_kernel, group),
        grid=(pieces // group,),
        out_shape=(
            jax.ShapeDtypeStruct((slots * PLANES, LANES), f32),
            jax.ShapeDtypeStruct((13, PLANES, LANES), f32),
        ),
        in_specs=[
            vmem, vmem, vmem, vmem,
        ],
        out_specs=(
            pl.BlockSpec((group * CHUNK * PLANES, LANES), lambda g: (g, 0)),
            pl.BlockSpec((13, PLANES, LANES), lambda g: (0, 0, 0)),
        ),
        compiler_params=pltpu.CompilerParams(vmem_limit_bytes=32 * 2**20),
        name="correct",
    )(updated, grad, change, settled)
    return out.reshape(slots, PLANES, LANES), moments


def solution(mesh):
    return jax.shard_map(
        functools.partial(local, mesh.shape["space"], mesh.shape["vel"]),
        mesh=mesh,
        in_specs=(
            P("vel", "space", None),
            P("vel"),
            P(None, "space", None),
            P("space", None),
            P("space", None),
        ),
        out_specs=(P("vel", "space", None), P(None, "space", None)),
        check_vma=False,
    )
```

```python
import functools
import math

import jax
import jax.numpy as jnp
import numpy as np
from jax import lax
from jax.experimental import pallas as pl
from jax.experimental.pallas import tpu as pltpu
from jax.sharding import PartitionSpec as P

SWEEPS = 4
LID_SPEED = 1.0
COUPLING = (
    (0, 1, 0, 0.24),
    (0, 2, 1, 0.24),
    (0, 3, 2, 0.24),
    (1, 0, 0, 0.2),
    (1, 4, 0, 0.2),
    (1, 5, 0, 0.2),
    (1, 7, 1, 0.1),
    (1, 8, 2, 0.1),
    (2, 0, 1, 0.2),
    (2, 4, 1, 0.2),
    (2, 6, 1, 0.2),
    (2, 7, 0, 0.1),
    (2, 9, 2, 0.1),
    (3, 0, 2, 0.2),
    (3, 4, 2, 0.2),
    (3, 8, 0, 0.1),
    (3, 9, 1, 0.1),
    (4, 10, 0, 0.2),
    (4, 11, 1, 0.2),
    (4, 12, 2, 0.2),
    (5, 1, 0, 0.4),
    (5, 10, 0, 0.2),
    (6, 2, 1, 0.4),
    (6, 11, 1, 0.2),
    (7, 1, 1, 0.2),
    (7, 2, 0, 0.2),
    (8, 1, 2, 0.2),
    (8, 3, 0, 0.2),
    (9, 2, 2, 0.2),
    (9, 3, 1, 0.2),
    (10, 4, 0, 0.5),
    (10, 5, 0, 0.2),
    (11, 4, 1, 0.5),
    (11, 6, 1, 0.2),
    (12, 4, 2, 0.5),
    (12, 8, 0, 0.1),
    (12, 9, 1, 0.1),
)


PLANES = 4
LANES = 128
SHIFT_Y = 8
SHIFT_Z = 1
CHUNK = 512
SUB = 256
COLS = 8
MESH = pl.DeviceIdType.MESH


def in_hbm(x):
    return pltpu.with_memory_space_constraint(x, pltpu.HBM)


def split(x):
    high = x.astype(jnp.bfloat16)
    low = (x - high.astype(jnp.float32)).astype(jnp.bfloat16)
    return high, low


def store_rows(ref, rows):
    for k, row in enumerate(rows):
        ref[pl.ds(k, 1), :] = row


def transport_kernel(
    n_space, n_vel, chunks,
    dist_ref, order_hbm, macro_hbm, rate_hbm, wall_hbm,
    upd, grad_ref, change_ref, mom_ref,
    order_ref, macro_ref, rate_ref, wall_ref,
    dist, halo, stage, table, eq_t, mom_t, rhs, rhs_f, acc, fields, fields_src,
    rs_src, rs_dst, reduced, held,
    small_sem, in_sem, halo_send, halo_recv, fld_send, fld_recv, rs_send, rs_recv, ag_send, ag_recv,
):
    space = lax.axis_index("space")
    vel = lax.axis_index("vel")
    has_left = space > 0
    has_right = space < n_space - 1
    rows_part = 16 * PLANES // n_vel
    per_plane = n_vel // PLANES

    small = [
        pltpu.make_async_copy(source, target, small_sem.at[k])
        for k, (source, target) in enumerate(
            (
                (rate_hbm, rate_ref), (wall_hbm, wall_ref), (macro_hbm, macro_ref),
                (order_hbm, order_ref),
            )
        )
    ]
    for copy in small:
        copy.start()

    def in_copy(i):
        rows = pl.ds(i * (CHUNK * PLANES), CHUNK * PLANES)
        return pltpu.make_async_copy(dist_ref.at[rows, :], dist.at[i], in_sem.at[i])

    def load_chunk(c, carry):
        in_copy(c).start()
        in_copy(chunks + c).start()
        return carry

    lax.fori_loop(0, chunks, load_chunk, 0)

    barrier = pltpu.get_barrier_semaphore()
    for off in range(n_vel):
        peer = lax.rem(vel + off, n_vel)
        if off:
            pl.semaphore_signal(barrier, inc=1, device_id={"vel": peer}, device_id_type=MESH)

        @pl.when(has_left)
        def _():
            pl.semaphore_signal(
                barrier, inc=1, device_id={"space": space - 1, "vel": peer}, device_id_type=MESH
            )

        @pl.when(has_right)
        def _():
            pl.semaphore_signal(
                barrier, inc=1, device_id={"space": space + 1, "vel": peer}, device_id_type=MESH
            )

    for copy in small[:3]:
        copy.wait()

    fields_src[0:4, :] = rate_ref[...]
    fields_src[4:8, :] = wall_ref[...].astype(jnp.float32)
    fields_src[8:12, :] = macro_ref[0]
    fields_src[12:16, :] = jnp.zeros((4, LANES), jnp.float32)

    @pl.when(jnp.logical_not(has_left))
    def _():
        fields[0] = jnp.zeros((16, LANES), jnp.float32)
        held[0] = jnp.zeros(held.shape[1:], jnp.float32)
        halo[0:chunks] = jnp.zeros((chunks, CHUNK, LANES), jnp.float32)

    @pl.when(jnp.logical_not(has_right))
    def _():
        fields[1] = jnp.zeros((16, LANES), jnp.float32)
        held[2] = jnp.zeros(held.shape[1:], jnp.float32)
        halo[chunks : 2 * chunks] = jnp.zeros((chunks, CHUNK, LANES), jnp.float32)

    beside = jnp.minimum(space, 1) + jnp.minimum(n_space - 1 - space, 1)
    pl.semaphore_wait(barrier, n_vel - 1 + n_vel * beside)

    def fields_copy(side):
        return pltpu.make_async_remote_copy(
            fields_src, fields.at[side], fld_send.at[side], fld_recv.at[side],
            device_id={"space": space + 1 if side == 0 else space - 1}, device_id_type=MESH,
        )

    def halo_copy(side, i):
        return pltpu.make_async_remote_copy(
            stage.at[i], halo.at[i], halo_send.at[i], halo_recv.at[i],
            device_id={"space": space + 1 if side == 0 else space - 1}, device_id_type=MESH,
        )

    sends = (has_right, has_left)
    receives = (has_left, has_right)
    for side in range(2):

        @pl.when(sends[side])
        def _():
            fields_copy(side).start()

    def send_halo(c, carry):
        for side in range(2):
            i = side * chunks + c
            in_copy(i).wait()
            plane = PLANES - 1 if side == 0 else 0

            @pl.when(sends[side])
            def _():
                stage[i] = dist[i, pl.ds(plane, CHUNK, stride=PLANES), :]
                halo_copy(side, i).start()

        return carry

    lax.fori_loop(0, chunks, send_halo, 0)

    small[3].wait()

    def make_tables(i, carry):
        order = order_ref[i]
        x = ((order >> 10) * 2 - 31).astype(jnp.float32) * 0.125
        y = (((order >> 5) & 31) * 2 - 31).astype(jnp.float32) * 0.125
        z = ((order & 31) * 2 - 31).astype(jnp.float32) * 0.125
        square = x * x + y * y + z * z
        one = jnp.ones_like(x)
        zero = jnp.zeros_like(x)
        energy = square - 1.5
        heat = square - 2.5
        store_rows(
            table,
            [one, x, y, z, energy, x * heat, y * heat, z * heat,
             zero, zero, zero, zero, zero, zero, zero, zero],
        )
        high, low = split(table[...])
        eq_t[i, 0:16, :] = high
        eq_t[i, 16:32, :] = low
        eq_t[i, 32:48, :] = high
        weight = jnp.exp(-square) * (0.25**3 / math.pi**1.5)
        third = square * (1.0 / 3.0)
        store_rows(
            table,
            [weight, weight * x, weight * y, weight * z, weight * energy * (2.0 / 3.0),
             2.0 * weight * (x * x - third), 2.0 * weight * (y * y - third),
             2.0 * weight * (x * y), 2.0 * weight * (x * z), 2.0 * weight * (y * z),
             weight * x * heat, weight * y * heat, weight * z * heat, zero, zero, zero],
        )
        high, low = split(table[...])
        mom_t[i, 0:16, :] = high
        mom_t[i, 16:32, :] = low
        store_rows(
            table,
            [one, 2.0 * x, 2.0 * y, 2.0 * z, energy, x * x - z * z, y * y - z * z,
             2.0 * x * y, 2.0 * x * z, 2.0 * y * z,
             0.8 * x * heat, 0.8 * y * heat, 0.8 * z * heat, zero, zero, zero],
        )
        high, low = split(table[...])
        grad_ref[i, 0:16, :] = high
        grad_ref[i, 16:32, :] = low
        grad_ref[i, 32:48, :] = high
        return carry

    lax.fori_loop(0, 2 * chunks, make_tables, 0)

    zero_row = jnp.zeros((1, LANES), jnp.float32)
    rhs_f[...] = jnp.zeros((16, COLS * LANES), jnp.float32)
    shakhov = 4.0 / 15.0
    for p in range(PLANES):
        rate = rate_ref[pl.ds(p, 1), :]
        wall = wall_ref[pl.ds(p, 1), :]
        gas = wall == 0
        moving = jnp.where(wall == 2, 2.0 * LID_SPEED, 0.0)
        for k, (source, scale) in enumerate(
            ((0, 1.0), (1, 2.0), (2, 2.0), (3, 2.0), (4, 1.0), (10, shakhov), (11, shakhov), (12, shakhov))
        ):
            value = macro_ref[source, pl.ds(p, 1), :]
            other = value if k == 0 else moving if k == 1 else zero_row
            rhs_f[pl.ds(k, 1), pl.ds(p * LANES, LANES)] = jnp.where(gas, rate * value * scale, other)
    for k in range(3):
        rhs_f[pl.ds(1 + k, 1), pl.ds((5 + k) * LANES, LANES)] = jnp.ones((1, LANES), jnp.float32)

    for side in range(2):

        @pl.when(receives[side])
        def _():
            fields_copy(side).wait_recv()

        plane = PLANES - 1 if side == 0 else 0
        wall_next = fields[side, pl.ds(4 + plane, 1), :]
        rhs_f[pl.ds(0, 1), pl.ds(4 * LANES, LANES)] = fields[side, pl.ds(8 + plane, 1), :]
        rhs_f[pl.ds(1, 1), pl.ds(4 * LANES, LANES)] = jnp.where(wall_next > 1.5, 2.0 * LID_SPEED, 0.0)
        high, low = split(rhs_f[...])
        rhs[side, 0:16, :] = high
        rhs[side, 16:32, :] = high
        rhs[side, 32:48, :] = low

    acc[...] = jnp.zeros(acc.shape, jnp.float32)

    def advance(side, i):
        @pl.when(receives[side])
        def _():
            halo_copy(side, i).wait_recv()

        for sub in range(CHUNK // SUB):
            first = sub * SUB
            lhs = eq_t[i, :, first : first + SUB]
            out = lax.dot_general(
                lhs, rhs[side], (((0,), (0,)), ((), ())), preferred_element_type=jnp.float32
            )
            cols = [out[:, k * LANES : (k + 1) * LANES] for k in range(COLS)]
            speed_x, speed_y, speed_z = (jnp.abs(col) for col in cols[5:8])
            up_y, up_z = cols[6] > 0, cols[7] > 0
            total = speed_x + speed_y + speed_z
            gas = [wall_ref[pl.ds(p, 1), :] == 0 for p in range(PLANES)]
            plane = PLANES - 1 if side == 0 else 0
            gas_next = fields[side, pl.ds(4 + plane, 1), :] == 0.0
            current = [
                jnp.where(gas[p], dist[i, pl.ds(first * PLANES + p, SUB, stride=PLANES), :], cols[p])
                for p in range(PLANES)
            ]
            beyond = jnp.where(gas_next, halo[i, first : first + SUB, :], cols[4])
            line = [beyond] + current[:-1] if side == 0 else current[1:] + [beyond]
            for p in range(PLANES):
                cells = current[p]
                along_y = jnp.where(
                    up_y, pltpu.roll(cells, SHIFT_Y, 1), pltpu.roll(cells, LANES - SHIFT_Y, 1)
                )
                along_z = jnp.where(
                    up_z, pltpu.roll(cells, SHIFT_Z, 1), pltpu.roll(cells, LANES - SHIFT_Z, 1)
                )
                flow = cols[p] + speed_x * line[p] + speed_y * along_y + speed_z * along_z
                below = total + rate_ref[pl.ds(p, 1), :]
                guess = pl.reciprocal(below, approx=True)
                guess = guess * (2.0 - below * guess)
                value = jnp.where(gas[p], flow * guess, cols[p])
                upd[i, p, first : first + SUB, :] = value
                high, low = split(value)
                acc[:, 2 * p * LANES : 2 * (p + 1) * LANES] += jnp.dot(
                    mom_t[i, :, first : first + SUB],
                    jnp.concatenate([high, low], axis=1),
                    preferred_element_type=jnp.float32,
                )

    near = 1 - lax.rem(space, 2)

    def step(k, carry):
        c = lax.rem(k, chunks)
        turn = lax.rem(k // chunks + near, 2)
        for side in range(2):

            @pl.when(turn == side)
            def _():
                advance(side, side * chunks + c)

        return carry

    lax.fori_loop(0, 2 * chunks, step, 0)

    for part in range(n_vel):
        plane, k = part // per_plane, part % per_plane
        first = k * rows_part
        tops, lows = pl.ds(first, rows_part), pl.ds(16 + first, rows_part)
        high, low = pl.ds(2 * plane * LANES, LANES), pl.ds((2 * plane + 1) * LANES, LANES)
        rs_src[part] = (acc[tops, high] + acc[tops, low]) + (acc[lows, high] + acc[lows, low])

    def rs_copy(off):
        peer = lax.rem(vel + off, n_vel)
        return pltpu.make_async_remote_copy(
            rs_src.at[peer], rs_dst.at[vel], rs_send.at[off], rs_recv.at[vel],
            device_id={"vel": peer}, device_id_type=MESH,
        )

    def rs_arrival(off):
        peer = lax.rem(vel + off, n_vel)
        return pltpu.make_async_remote_copy(
            rs_src.at[peer], rs_dst.at[peer], rs_send.at[off], rs_recv.at[peer],
            device_id={"vel": peer}, device_id_type=MESH,
        )

    for off in range(1, n_vel):
        rs_copy(off).start()
    rs_dst[vel] = rs_src[vel]
    for off in range(1, n_vel):
        rs_arrival(off).wait_recv()
    whole = rs_dst[0]
    for part in range(1, n_vel):
        whole = whole + rs_dst[part]
    reduced[...] = whole

    def ag_copy(shift, off):
        return pltpu.make_async_remote_copy(
            reduced, held.at[1 - shift, vel],
            ag_send.at[1 + shift, off], ag_recv.at[1 - shift, vel],
            device_id={"space": space + shift, "vel": lax.rem(vel + off, n_vel)}, device_id_type=MESH,
        )

    def ag_arrival(k, off):
        peer = lax.rem(vel + off, n_vel)
        return pltpu.make_async_remote_copy(
            reduced, held.at[k, peer],
            ag_send.at[k, off], ag_recv.at[k, peer],
            device_id={"space": space, "vel": peer}, device_id_type=MESH,
        )

    @pl.when(has_left)
    def _():
        for off in range(n_vel):
            ag_copy(-1, off).start()

    @pl.when(has_right)
    def _():
        for off in range(n_vel):
            ag_copy(1, off).start()

    for off in range(1, n_vel):
        ag_copy(0, off).start()
    held[1, vel] = whole
    for off in range(1, n_vel):
        ag_arrival(1, off).wait_recv()

    @pl.when(has_left)
    def _():
        for off in range(n_vel):
            ag_arrival(0, off).wait_recv()

    @pl.when(has_right)
    def _():
        for off in range(n_vel):
            ag_arrival(2, off).wait_recv()

    start = []
    for k in range(3):
        for p in range(PLANES):
            parts = [held[k, p * per_plane + m] for m in range(per_plane)]
            start.append(parts[0] if per_plane == 1 else jnp.concatenate(parts, axis=0))
    reaction, gas = [], []
    for k in range(3):
        for p in range(PLANES):
            source = fields_src if k == 1 else fields.at[0 if k == 0 else 1]
            reaction.append(1.0 + source[pl.ds(p, 1), :])
            gas.append(source[pl.ds(4 + p, 1), :] == 0.0)
    now = list(start)
    row = lax.broadcasted_iota(jnp.int32, (16, 48), 0)
    column = lax.broadcasted_iota(jnp.int32, (16, 48), 1)
    weight = jnp.zeros((16, 48), jnp.float32)
    for into, source, dim, value in COUPLING:
        weight = jnp.where((row == into) & (column == dim * 16 + source), value, weight)
    high, low = split(weight)
    coupling = jnp.concatenate([high, low, high], axis=1)
    count = len(start)
    for sweep in range(1, SWEEPS + 1):
        inner = range(sweep, count - sweep)
        sums, differences = [], []
        for p in inner:
            up_y = pltpu.roll(now[p], LANES - SHIFT_Y, 1)
            down_y = pltpu.roll(now[p], SHIFT_Y, 1)
            up_z = pltpu.roll(now[p], LANES - SHIFT_Z, 1)
            down_z = pltpu.roll(now[p], SHIFT_Z, 1)
            sums.append(now[p + 1] + now[p - 1] + up_y + down_y + up_z + down_z)
            differences.append(
                jnp.concatenate([now[p + 1] - now[p - 1], up_y - down_y, up_z - down_z], axis=0)
            )
        high, low = split(jnp.concatenate(differences, axis=1))
        coupled = jnp.dot(
            coupling,
            jnp.concatenate([high, high, low], axis=0),
            preferred_element_type=jnp.float32,
        )
        later = list(now)
        for m, p in enumerate(inner):
            value = reaction[p] * start[p] + sums[m] - 0.5 * coupled[:, m * LANES : (m + 1) * LANES]
            later[p] = jnp.where(gas[p], value / (reaction[p] + 6.0), start[p])
        now = later

    for p in range(PLANES):
        lanes = pl.ds(p * LANES, LANES)
        high, low = split(now[PLANES + p] - start[PLANES + p])
        change_ref[0:16, lanes] = high
        change_ref[16:32, lanes] = high
        change_ref[32:48, lanes] = low
        for k in range(13):
            mom_ref[k, pl.ds(p, 1), :] = now[PLANES + p][k : k + 1, :]

    def drain(c, carry):
        for side in range(2):
            i = side * chunks + c
            @pl.when(sends[side])
            def _():
                halo_copy(side, i).wait_send()

        return carry

    lax.fori_loop(0, chunks, drain, 0)
    for side in range(2):

        @pl.when(sends[side])
        def _():
            fields_copy(side).wait_send()

    for off in range(1, n_vel):
        rs_copy(off).wait_send()
        ag_copy(0, off).wait_send()

    @pl.when(has_left)
    def _():
        for off in range(n_vel):
            ag_copy(-1, off).wait_send()

    @pl.when(has_right)
    def _():
        for off in range(n_vel):
            ag_copy(1, off).wait_send()


def correct_kernel(group, upd_ref, grad_ref, change_ref, settled_ref, out_ref, mom_ref):
    @pl.when(pl.program_id(0) == 0)
    def _():
        mom_ref[...] = settled_ref[...]

    base = pl.program_id(0) * group
    for i in range(group):
        change = lax.dot_general(
            grad_ref[base + i], change_ref[...], (((0,), (0,)), ((), ())), preferred_element_type=jnp.float32
        )
        for p in range(PLANES):
            rows = pl.ds(i * CHUNK * PLANES + p, CHUNK, stride=PLANES)
            out_ref[rows, :] = upd_ref[base + i, p] + change[:, p * LANES : (p + 1) * LANES]


def local(n_space, n_vel, distribution, velocity_order, macro_state, rarefaction, wall_mask):
    slots = distribution.shape[0]
    pieces = slots // CHUNK
    chunks = pieces // 2
    f32, bf16 = jnp.float32, jnp.bfloat16
    rows_part = 16 * PLANES // n_vel
    vmem = pl.BlockSpec(memory_space=pltpu.VMEM)
    hbm = pl.BlockSpec(memory_space=pltpu.HBM)
    dma = pltpu.SemaphoreType.DMA
    updated, grad, change, settled = pl.pallas_call(
        functools.partial(transport_kernel, n_space, n_vel, chunks),
        out_shape=(
            jax.ShapeDtypeStruct((pieces, PLANES, CHUNK, LANES), f32),
            jax.ShapeDtypeStruct((pieces, 48, CHUNK), bf16),
            jax.ShapeDtypeStruct((48, PLANES * LANES), bf16),
            jax.ShapeDtypeStruct((13, PLANES, LANES), f32),
        ),
        in_specs=[hbm] * 5,
        out_specs=(vmem,) * 4,
        scratch_shapes=[
            pltpu.VMEM((pieces, 1, CHUNK), jnp.int32),
            pltpu.VMEM((13, PLANES, LANES), f32),
            pltpu.VMEM((PLANES, LANES), f32),
            pltpu.VMEM((PLANES, LANES), jnp.int32),
            pltpu.VMEM((pieces, CHUNK * PLANES, LANES), f32),
            pltpu.VMEM((pieces, CHUNK, LANES), f32),
            pltpu.VMEM((pieces, CHUNK, LANES), f32),
            pltpu.VMEM((16, CHUNK), f32),
            pltpu.VMEM((pieces, 48, CHUNK), bf16),
            pltpu.VMEM((pieces, 32, CHUNK), bf16),
            pltpu.VMEM((2, 48, COLS * LANES), bf16),
            pltpu.VMEM((16, COLS * LANES), f32),
            pltpu.VMEM((32, 2 * PLANES * LANES), f32),
            pltpu.VMEM((2, 16, LANES), f32),
            pltpu.VMEM((16, LANES), f32),
            pltpu.VMEM((n_vel, rows_part, LANES), f32),
            pltpu.VMEM((n_vel, rows_part, LANES), f32),
            pltpu.VMEM((rows_part, LANES), f32),
            pltpu.VMEM((3, n_vel, rows_part, LANES), f32),
            dma((4,)), dma((pieces,)), dma((pieces,)), dma((pieces,)),
            dma((2,)), dma((2,)), dma((n_vel,)), dma((n_vel,)), dma((3, n_vel)), dma((3, n_vel)),
        ],
        compiler_params=pltpu.CompilerParams(
            collective_id=0, has_side_effects=True, vmem_limit_bytes=40 * 2**20
        ),
        name="transport",
    )(
        distribution.reshape(slots * PLANES, LANES),
        in_hbm(velocity_order.reshape(pieces, 1, CHUNK)),
        in_hbm(macro_state),
        in_hbm(rarefaction),
        in_hbm(wall_mask),
    )
    group = 2
    out, moments = pl.pallas_call(
        functools.partial(correct_kernel, group),
        grid=(pieces // group,),
        out_shape=(
            jax.ShapeDtypeStruct((slots * PLANES, LANES), f32),
            jax.ShapeDtypeStruct((13, PLANES, LANES), f32),
        ),
        in_specs=[
            vmem, vmem, vmem, vmem,
        ],
        out_specs=(
            pl.BlockSpec((group * CHUNK * PLANES, LANES), lambda g: (g, 0)),
            pl.BlockSpec((13, PLANES, LANES), lambda g: (0, 0, 0)),
        ),
        compiler_params=pltpu.CompilerParams(vmem_limit_bytes=32 * 2**20),
        name="correct",
    )(updated, grad, change, settled)
    return out.reshape(slots, PLANES, LANES), moments


def solution(mesh):
    return jax.shard_map(
        functools.partial(local, mesh.shape["space"], mesh.shape["vel"]),
        mesh=mesh,
        in_specs=(
            P("vel", "space", None),
            P("vel"),
            P(None, "space", None),
            P("space", None),
            P("space", None),
        ),
        out_specs=(P("vel", "space", None), P(None, "space", None)),
        check_vma=False,
    )
```
